32 devices in a mesh: row: 4 (over x, core), mp: 8 (over z, y).
Axes of the slice: x: 2, y: 2, z: 4, core: 2. Of those that a mesh axis runs over, the one named last changes fastest.
Arguments:
- queries: bfloat16 [1280, 16384], P('row', 'mp'), may hold values from -16 to 16
- new_kv: bfloat16 [1280, 2048], P('row', 'mp'), may hold values from -9 to 9
- cache_keys: bfloat16 [256, 16, 512, 128], P('row', 'mp'), may hold values from -26 to 26
- cache_values: bfloat16 [256, 16, 512, 128], P('row', 'mp'), may hold values from -12 to 12
- cache_lens: int32 [256], P('row'), may hold values from 8 to 1019, as said below
- accepted: int32 [256], P('row'), may hold values from 0 to 5
- dest: int32 [256], P('row'), may hold values from 0 to 255, as said below
- out_weight: bfloat16 [16384, 16384], P('mp', 'row'), may hold values from -0.046875 to 0.046875
Outputs:
- mixed: bfloat16 [1280, 16384], P('mp', 'row')
- next_kv: bfloat16 [256, 5, 2048], P('row', None, 'mp')
The draws below stay inside these ranges and needn't reach their ends.
Inputs may be any that keep to these rules, and one draw needn't show every extreme that they name: `cache_lens`: every beam's cache leaves room for its 5 new tokens. dest is a permutation of 0 to 255; of the beams in each aligned block of 64 beams, exactly 16 go to slots of each aligned block of 64 slots.
All inputs are finite; a program needn't handle non-finite values.
Results may differ from the reference program's by a relative error of at most 0.02.
Values may be sent and summed in bfloat16 or wider, within the bound.
No kernel may reach another device: no remote copies, remote signals or barrier semaphores. Data moves between devices by JAX's collectives and lax.ppermute only.
A program may use at most 128 MiB of HBM per device.

```python
import jax
import jax.numpy as jnp
from jax import lax

D = 16384
HQ = 128
KVH = 8
HD = 128
GROUP = 16
DRAFT = 5
CACHE = 1024
HALF = 512
BEAMS_ROW = 64
BEAMS = 256
TOKENS = 1280
SHARE = 16


def draw_queries(key, part):
    main_key = jax.random.fold_in(key, 3)
    shape = (BEAMS, DRAFT, KVH, HQ // KVH, HD)
    values = jnp.clip(jax.random.normal(main_key, shape, jnp.float32), -6.0, 6.0)
    return values.reshape(TOKENS, HQ * HD).astype(jnp.bfloat16)


def draw_cache_keys(key, part):
    main_key = jax.random.fold_in(key, 5)
    shape = (BEAMS, KVH, 2, HALF, HD)
    values = 1.5 * jnp.clip(jax.random.normal(main_key, shape, jnp.float32), -6.0, 6.0)
    return values.reshape(BEAMS, 2 * KVH, HALF, HD).astype(jnp.bfloat16)


def draw_cache_lens(key, part):
    base_key = jax.random.fold_in(key, 7)
    key_one, key_two, key_three = jax.random.split(base_key, 3)
    top_bits = CACHE.bit_length()
    powers = jax.random.randint(key_one, (BEAMS,), 3, top_bits)
    lower = jnp.left_shift(jnp.int32(1), powers.astype(jnp.int32))
    lengths = jax.random.randint(key_two, (BEAMS,), lower, 2 * lower)
    lengths = jnp.minimum(lengths, CACHE - DRAFT).astype(jnp.int32)
    picked = jax.random.randint(key_three, (), 0, BEAMS)
    lengths = lengths.at[picked].set(CACHE - DRAFT)
    lengths = lengths.at[(picked + 1) % BEAMS].set(8)
    return lengths.astype(jnp.int32)


def draw_dest(key, part):
    base_key = jax.random.fold_in(key, 9)
    key_one, key_two = jax.random.split(base_key)
    blocks = BEAMS_ROW // SHARE
    send_keys = jax.random.split(key_one, blocks)
    land_keys = jax.random.split(key_two, blocks)
    send_order = jax.vmap(lambda k: jax.random.permutation(k, BEAMS_ROW))(send_keys)
    land_order = jax.vmap(lambda k: jax.random.permutation(k, BEAMS_ROW))(land_keys)
    ranks = jnp.argsort(send_order, axis=1).astype(jnp.int32)
    target = ranks // SHARE
    within = ranks % SHARE
    source = jnp.arange(blocks, dtype=jnp.int32)[:, None]
    landing = land_order[target, source * SHARE + within]
    slots = target * BEAMS_ROW + landing
    return slots.reshape(BEAMS).astype(jnp.int32)


def set_ends(values, own_key, smallest, largest):
    index_at = [jax.random.randint(jax.random.fold_in(own_key, axis), (), 0, length) for axis, length in enumerate(values.shape)]
    longest = values.shape.index(max(values.shape))
    neighbour = index_at[:longest] + [(index_at[longest] + 1) % values.shape[longest]] + index_at[longest + 1:]
    return values.at[tuple(index_at)].set(smallest).at[tuple(neighbour)].set(largest)


def block_levels(rng, extent, pieces, least, largest):
    factor_of, own = 1.0, jax.random.fold_in(rng, 6)
    for axis_at, blocks in pieces:
        steps = jnp.exp(jax.random.uniform(jax.random.fold_in(own, axis_at), (blocks,), jnp.float32, least / len(pieces), largest / len(pieces)))
        factor_of = factor_of * jnp.repeat(steps, extent[axis_at] // blocks).reshape([-1 if axis == axis_at else 1 for axis in range(len(extent))])
    return factor_of


def gaussian(own_key, shape, scale, most, cuts=(), kind=jnp.bfloat16):
    array = scale * jax.random.normal(own_key, shape, jnp.float32)
    if cuts:
        array = array * block_levels(own_key, shape, cuts, -0.22, 0.18)
    return jnp.clip(array, -most, most).astype(kind)


def setup_inputs(seed: int = 0) -> dict:
    seeds = jax.random.split(jax.random.key(seed), 9)
    queries = draw_queries(jax.random.fold_in(seeds[8], 71), 0)
    new_kv = gaussian(seeds[1], (TOKENS, 2 * KVH * HD), 1.5, 9.0, ((0, 4), (1, 8)))
    cache_keys = draw_cache_keys(jax.random.fold_in(seeds[8], 71), 0)
    cache_values = gaussian(seeds[3], (BEAMS, 2 * KVH, HALF, HD), 2.0, 12.0, ((0, 4), (1, 8)))
    cache_lens = draw_cache_lens(jax.random.fold_in(seeds[8], 71), 0)
    accepted = set_ends(jax.random.randint(seeds[5], (BEAMS,), 0, DRAFT + 1), jax.random.fold_in(seeds[5], 1), 0, DRAFT).astype(jnp.int32)
    dest = draw_dest(jax.random.fold_in(seeds[8], 71), 0)
    out_weight = gaussian(seeds[7], (HQ * HD, D), (HQ * HD) ** -0.5, 0.046875, ((0, 8), (1, 4)))
    return {"queries": queries, "new_kv": new_kv, "cache_keys": cache_keys, "cache_values": cache_values, "cache_lens": cache_lens, "accepted": accepted, "dest": dest, "out_weight": out_weight}


masked_score = -1e30


def beam_attention(inputs):
    beam_queries, beam_fresh, beam_keys, beam_values, length = inputs
    scale = HD ** -0.5
    query_block = beam_queries.astype(jnp.float32).reshape(DRAFT, KVH, GROUP, HD).transpose(1, 0, 2, 3)
    key_block = beam_keys.astype(jnp.float32).reshape(KVH, 2, HALF, HD)
    value_block = beam_values.astype(jnp.float32).reshape(KVH, 2, HALF, HD)
    fresh_block = beam_fresh.astype(jnp.float32).reshape(DRAFT, KVH, 2, HD).transpose(1, 0, 2, 3)
    fresh_keys = fresh_block[:, :, 0]
    fresh_values = fresh_block[:, :, 1]
    cache_scores = jnp.einsum("gtjd,gsid->gstji", query_block, key_block) * scale
    fresh_scores = jnp.einsum("gtjd,gud->gtju", query_block, fresh_keys) * scale
    halves = jnp.arange(2, dtype=jnp.int32)
    spots = halves[:, None] * HALF + jnp.arange(HALF, dtype=jnp.int32)[None, :]
    cache_valid = spots < length
    order = jnp.arange(DRAFT, dtype=jnp.int32)
    fresh_side = (length + order) // HALF
    fresh_valid = (order[None, :, None] >= order[None, None, :]) & (fresh_side[None, None, :] == halves[:, None, None])
    scores = jnp.concatenate([cache_scores, jnp.broadcast_to(fresh_scores[:, None], (KVH, 2, DRAFT, GROUP, DRAFT))], axis=-1)
    valid = jnp.concatenate([jnp.broadcast_to(cache_valid[None, :, None, None, :], (KVH, 2, DRAFT, GROUP, HALF)), jnp.broadcast_to(fresh_valid[None, :, :, None, :], (KVH, 2, DRAFT, GROUP, DRAFT))], axis=-1)
    masked = jnp.where(valid, scores, masked_score)
    highest = jnp.max(masked, axis=-1)
    weights = jnp.where(valid, jnp.exp(masked - highest[..., None]), 0.0).astype(jnp.bfloat16)
    weights_wide = weights.astype(jnp.float32)
    values_all = jnp.concatenate([value_block, jnp.broadcast_to(fresh_values[:, None], (KVH, 2, DRAFT, HD))], axis=2)
    partial_value = jnp.einsum("gstju,gsud->gstjd", weights_wide, values_all)
    weight_mass = jnp.sum(weights_wide, axis=-1)
    summit = jnp.max(highest, axis=1)
    factor = jnp.exp(highest - summit[:, None])
    numer = jnp.sum(factor[..., None] * partial_value, axis=1)
    denom = jnp.sum(factor * weight_mass, axis=1)
    attention = (numer / denom[..., None]).astype(jnp.bfloat16)
    return attention.transpose(1, 0, 2, 3).reshape(DRAFT, HQ * HD)


def reference(queries, new_kv, cache_keys, cache_values, cache_lens, accepted, dest, out_weight):
    beam_queries = queries.reshape(BEAMS, DRAFT, HQ * HD)
    beam_fresh = new_kv.reshape(BEAMS, DRAFT, 2 * KVH * HD)
    attention = lax.map(beam_attention, (beam_queries, beam_fresh, cache_keys, cache_values, cache_lens))
    attention = attention.reshape(TOKENS, HQ * HD)
    mixed = jnp.dot(attention, out_weight, preferred_element_type=jnp.float32).astype(jnp.bfloat16)
    order = jnp.arange(DRAFT, dtype=jnp.int32)
    kept_mask = order[None, :] < accepted[:, None]
    kept_rows = jnp.where(kept_mask[..., None], beam_fresh, jnp.zeros_like(beam_fresh))
    next_kv = jnp.zeros_like(beam_fresh).at[dest].set(kept_rows)
    return mixed, next_kv
```

```python
import functools

import jax
import jax.numpy as jnp
from jax import lax
from jax.experimental import pallas as pl
from jax.experimental.pallas import tpu as pltpu
from jax.sharding import PartitionSpec as P

masked_score = -1e30
vmem_bytes = 60 * 2**20
early_beams = 8


def partner(block, axis, bit):
    count = lax.axis_size(axis)
    route = []
    for low in range(count):
        high = low | 1 << bit
        if high != low and high < count:
            route += [(low, high), (high, low)]
    return lax.ppermute(block, axis, route)


def head_slice(values, start, count):
    return lax.dynamic_slice_in_dim(values, start, count, 3)


def attention_kernel(scale, first, count, drafts, batch, group, lens, q, k, v, fresh, out,
                     q_raw, q_wide, f_wide, o_wide, k_held, v_held, order, q_sems, k_sems, v_sems):
    halves = out.shape[0]
    size = k.shape[2]
    span = k.shape[1]
    heads = q.shape[1] // size
    stride = k.shape[0] // halves
    block = 2 * size
    most = span // block
    batches = halves * count // batch
    per_half = count // batch
    low = first * drafts // 16 * 16
    shift = first * drafts - low
    taken = q_raw.shape[1]
    rows = heads * 8

    def start_of(n):
        return n // per_half * stride + first + n % per_half * batch

    def copies(n):
        beams = pl.ds(start_of(n), batch)
        slot = n
        return (
            pltpu.make_async_copy(k.at[beams], k_held.at[slot], k_sems.at[slot]),
            pltpu.make_async_copy(v.at[beams], v_held.at[slot], v_sems.at[slot]),
        )

    def query_copy(h):
        start = h * stride * drafts + low
        return pltpu.make_async_copy(q.at[pl.ds(start, taken)], q_raw.at[h], q_sems.at[h])

    for h in range(halves):
        query_copy(h).start()
    ahead = min(2, batches)
    for n in range(ahead):
        for copy in copies(n):
            copy.start()
    for side in range(2):
        f_wide[side, : fresh.shape[0]] = fresh[:, side * size : (side + 1) * size].astype(jnp.float32)
        f_wide[side, fresh.shape[0] :] = jnp.zeros((8, size), jnp.float32)
    for h in range(halves):
        query_copy(h).wait()
        for j in range(heads):
            q_wide[j, h, :taken] = q_raw[h, :, j * size : (j + 1) * size].astype(jnp.float32)
            q_wide[j, h, taken:] = jnp.zeros((8, size), jnp.float32)

    draft = lax.broadcasted_iota(jnp.int32, (2 * rows, 1), 0) % 8
    window = 32
    spot = lax.broadcasted_iota(jnp.int32, (window, 1), 0)
    contract = (((1,), (1,)), ((), ()))
    blank = jnp.zeros((rows, size), jnp.bfloat16)

    def blocks_of(beam):
        return (lens[beam] + (drafts + block - 1)) // block

    def attend_group(n, g, c):
        width = c * block
        for pair in range(group // 2):
            parts = []
            for m in range(2):
                i = order[g * group + 2 * pair + m]
                beam = start_of(n) + i
                length = lens[beam]
                at = pl.multiple_of(jnp.minimum(length // 16 * 16, width - window), 16)
                there = length - at
                inside = (spot >= there) & (spot < there + drafts)
                for side, held in enumerate((k_held, v_held)):
                    new = f_wide[side, pl.ds(beam * drafts, 8), :]
                    new = jnp.concatenate([new, jnp.zeros((window - 8, size), jnp.float32)], 0)
                    new = pltpu.roll(new, there, 0).astype(jnp.bfloat16)
                    old = held[n, i, pl.ds(at, window), :]
                    held[n, i, pl.ds(at, window), :] = jnp.where(inside, new, old)
                row = shift + (beam - start_of(n) + n % per_half * batch) * drafts
                qi = q_wide[:, n // per_half, pl.ds(row, 8), :].reshape(rows, size).astype(jnp.bfloat16)
                parts.append((i, length, row, qi))
            (i, length, row, qi), (i2, length2, row2, qi2) = parts
            left = jnp.concatenate(
                [jnp.concatenate([qi, blank], 1), jnp.concatenate([blank, qi2], 1)], 0
            )
            keys = jnp.concatenate([k_held[n, i, :width], k_held[n, i2, :width]], 1)
            s = lax.dot_general(left, keys, contract, preferred_element_type=jnp.float32)
            which = lax.broadcasted_iota(jnp.int32, (2 * rows, 1), 0) < rows
            limit = jnp.where(which, length, length2) + draft
            s = jnp.where(lax.broadcasted_iota(jnp.int32, (1, width), 1) <= limit, s, masked_score)
            top = jnp.max(s, 1, keepdims=True)
            w = jnp.exp((s - top) * scale).astype(jnp.bfloat16)
            mass = jnp.sum(w.astype(jnp.float32), 1, keepdims=True)
            values = jnp.concatenate([v_held[n, i, :width], v_held[n, i2, :width]], 1)
            total = jnp.dot(w, values, preferred_element_type=jnp.float32)
            share = 1.0 / mass
            for m, start in ((0, row), (1, row2)):
                part = total[m * rows : (m + 1) * rows, m * size : (m + 1) * size]
                part = part * share[m * rows : (m + 1) * rows]
                o_wide[:, n // per_half, pl.ds(start - shift, drafts), :] = part.reshape(heads, 8, size)[:, :drafts]

    def step(n, carry):
        @pl.when(n + ahead < batches)
        def _():
            for copy in copies(jnp.minimum(n + ahead, batches - 1)):
                copy.start()

        held = [blocks_of(start_of(n) + m) for m in range(batch)]
        for m in range(batch):
            rank = jnp.int32(0)
            for other in range(batch):
                if other < m:
                    rank += (held[other] <= held[m]).astype(jnp.int32)
                elif other > m:
                    rank += (held[other] < held[m]).astype(jnp.int32)
            order[rank] = m
        for copy in copies(n):
            copy.wait()
        for g in range(batch // group):
            most_held = blocks_of(start_of(n) + order[g * group + group - 1])
            for c in range(1, most + 1):
                pl.when(most_held == c)(functools.partial(attend_group, n, g, c))
        return carry

    lax.fori_loop(0, batches, step, 0)
    for h in range(halves):
        for j in range(heads):
            out[h, :, j * size : (j + 1) * size] = o_wide[j, h].astype(out.dtype)


def attend(q, k, v, fresh, lens, first, count, halves, drafts, batch=8, group=4):
    beams, size = k.shape[0], k.shape[3]
    span = k.shape[1] * k.shape[2]
    columns = q.shape[1]
    heads = columns // size
    stride = beams // halves
    taken = (first + count) * drafts - first * drafts // 16 * 16
    taken = (taken + 15) // 16 * 16
    batches = halves * count // batch
    full = pl.BlockSpec(memory_space=pltpu.VMEM)
    outside = pl.BlockSpec(memory_space=pl.ANY)
    return pl.pallas_call(
        functools.partial(attention_kernel, size**-0.5, first, count, drafts, batch, group),
        out_shape=jax.ShapeDtypeStruct((halves, count * drafts, columns), jnp.bfloat16),
        in_specs=[pl.BlockSpec(memory_space=pltpu.SMEM), outside, outside, outside, full],
        out_specs=full,
        scratch_shapes=[
            pltpu.VMEM((halves, taken, columns), jnp.bfloat16),
            pltpu.VMEM((heads, halves, taken + 8, size), jnp.float32),
            pltpu.VMEM((2, fresh.shape[0] + 8, size), jnp.float32),
            pltpu.VMEM((heads, halves, count * drafts, size), jnp.float32),
            pltpu.VMEM((batches, batch, span, size), jnp.bfloat16),
            pltpu.VMEM((batches, batch, span, size), jnp.bfloat16),
            pltpu.SMEM((batch,), jnp.int32),
            pltpu.SemaphoreType.DMA((halves,)),
            pltpu.SemaphoreType.DMA((batches,)),
            pltpu.SemaphoreType.DMA((batches,)),
        ],
        compiler_params=pltpu.CompilerParams(vmem_limit_bytes=vmem_bytes),
        cost_estimate=pl.CostEstimate(
            flops=4 * halves * count * drafts * columns * span,
            bytes_accessed=4 * halves * count * size * span,
            transcendentals=halves * count * drafts * heads * span,
        ),
    )(lens, q, k.reshape(beams, span, size), v.reshape(beams, span, size), fresh)


def half_attention(queries, new_kv, cache_keys, cache_values, cache_lens):
    beams_here, halves_held, half_length, head_size = cache_keys.shape
    drafts = queries.shape[0] // beams_here
    heads_owned = queries.shape[1] // head_size
    mp_place = lax.axis_index("mp")
    lower_side = mp_place % 2 == 0
    partner_queries, partner_fresh = partner((queries, new_kv), "mp", 0)
    group_queries = jnp.where(
        lower_side,
        jnp.concatenate([queries, partner_queries], 1),
        jnp.concatenate([partner_queries, queries], 1),
    )
    fresh_pair = jnp.where(
        lower_side,
        jnp.concatenate([new_kv, partner_fresh], 1),
        jnp.concatenate([partner_fresh, new_kv], 1),
    )
    group_heads = group_queries.shape[1] // head_size
    sides = (mp_place * halves_held + jnp.arange(halves_held, dtype=jnp.int32)) % 2
    query_block = group_queries.reshape(beams_here, drafts, group_heads, head_size)
    fresh_block = fresh_pair.reshape(beams_here, drafts, 2, head_size)
    fresh_keys = fresh_block[:, :, 0]
    fresh_values = fresh_block[:, :, 1]
    scale = head_size ** (-0.5)
    cache_scores = (
        jnp.einsum("btjd,bsid->bstji", query_block, cache_keys, preferred_element_type=jnp.float32)
        * scale
    )
    fresh_scores = (
        jnp.einsum("btjd,bud->btju", query_block, fresh_keys, preferred_element_type=jnp.float32)
        * scale
    )
    spots = sides[:, None] * half_length + jnp.arange(half_length, dtype=jnp.int32)[None, :]
    cache_valid = (spots[None] < cache_lens[:, None, None])[:, :, None, None, :]
    order = jnp.arange(drafts, dtype=jnp.int32)
    fresh_side = (cache_lens[:, None] + order[None, :]) // half_length
    causal = order[:, None] >= order[None, :]
    fresh_valid = (
        causal[None, None] & (fresh_side[:, None, None, :] == sides[None, :, None, None])
    )[:, :, :, None, :]
    cache_masked = jnp.where(cache_valid, cache_scores, masked_score)
    fresh_masked = jnp.where(fresh_valid, fresh_scores[:, None], masked_score)
    highest = jnp.maximum(jnp.max(cache_masked, -1), jnp.max(fresh_masked, -1))
    cache_weights = jnp.where(cache_valid, jnp.exp(cache_masked - highest[..., None]), 0.0).astype(
        jnp.bfloat16
    )
    fresh_weights = jnp.where(fresh_valid, jnp.exp(fresh_masked - highest[..., None]), 0.0).astype(
        jnp.bfloat16
    )
    partial_value = jnp.einsum(
        "bstji,bsid->bstjd", cache_weights, cache_values, preferred_element_type=jnp.float32
    )
    partial_value = partial_value + jnp.einsum(
        "bstju,bud->bstjd", fresh_weights, fresh_values, preferred_element_type=jnp.float32
    )
    weight_mass = jnp.sum(cache_weights.astype(jnp.float32), -1) + jnp.sum(
        fresh_weights.astype(jnp.float32), -1
    )
    own_start = jnp.where(lower_side, 0, heads_owned).astype(jnp.int32)
    other_start = (heads_owned - own_start).astype(jnp.int32)
    got_partial, got_highest, got_mass = partner(
        (
            head_slice(partial_value, other_start, heads_owned),
            head_slice(highest, other_start, heads_owned),
            head_slice(weight_mass, other_start, heads_owned),
        ),
        "mp",
        0,
    )
    both_partial = jnp.concatenate(
        [head_slice(partial_value, own_start, heads_owned), got_partial], 1
    )
    both_highest = jnp.concatenate([head_slice(highest, own_start, heads_owned), got_highest], 1)
    both_mass = jnp.concatenate([head_slice(weight_mass, own_start, heads_owned), got_mass], 1)
    summit = jnp.max(both_highest, 1)
    factor = jnp.exp(both_highest - summit[:, None])
    numer = jnp.sum(factor[..., None] * both_partial, 1)
    denom = jnp.sum(factor * both_mass, 1)
    return (
        (numer / denom[..., None])
        .astype(jnp.bfloat16)
        .reshape(beams_here * drafts, heads_owned * head_size)
    )


def gather_rows(block):
    count = lax.axis_size("row")
    if count != 4:
        return [lax.all_gather(block, "row", axis=0, tiled=False)[j] for j in range(count)]
    near = partner(block, "row", 0)
    far = partner(block, "row", 1)
    return [block, near, far, partner(far, "row", 0)]


def project_kernel(gathered, pieces, table, *refs):
    blocks, weight = refs[:gathered], refs[gathered]
    out, held = refs[gathered + 1 : -1], refs[-1]
    rows = blocks[0].shape[1]
    places = held.shape[0] // rows

    @pl.when(pl.program_id(0) == 0)
    def _():
        for at, block in enumerate(blocks):
            for piece in range(pieces):
                place = table[at * pieces + piece]
                for spot in range(places):

                    @pl.when(place == spot)
                    def _():
                        held[pl.ds(spot * rows, rows)] = block[piece]

    total = jnp.dot(held[...], weight[...], preferred_element_type=jnp.float32)
    if len(out) == 1:
        out[0][...] = total.astype(out[0].dtype)
    else:
        for spot in range(places):
            out[spot][...] = total[spot * rows : (spot + 1) * rows].astype(out[spot].dtype)


def project(table, blocks, weight, side, sides, apart):
    pieces, rows, depth = blocks[0].shape
    columns = weight.shape[1] // sides
    tile = min(512, columns)
    tiles = columns // tile
    places = pieces * len(blocks)
    if apart:
        out_shape = [jax.ShapeDtypeStruct((rows, columns), jnp.bfloat16)] * places
        out_specs = [pl.BlockSpec((rows, tile), lambda n, t: (0, n))] * places
    else:
        out_shape = jax.ShapeDtypeStruct((places * rows, columns), jnp.bfloat16)
        out_specs = pl.BlockSpec((places * rows, tile), lambda n, t: (0, n))
    return pl.pallas_call(
        functools.partial(project_kernel, len(blocks), pieces),
        out_shape=out_shape,
        grid_spec=pltpu.PrefetchScalarGridSpec(
            num_scalar_prefetch=1,
            grid=(tiles,),
            in_specs=[pl.BlockSpec((pieces, rows, depth), lambda n, t: (0, 0, 0))] * len(blocks)
            + [pl.BlockSpec((depth, tile), lambda n, t: (0, n + side * tiles))],
            out_specs=out_specs,
            scratch_shapes=[pltpu.VMEM((places * rows, depth), jnp.bfloat16)],
        ),
        compiler_params=pltpu.CompilerParams(vmem_limit_bytes=vmem_bytes),
        cost_estimate=pl.CostEstimate(
            flops=2 * places * rows * depth * columns,
            bytes_accessed=2 * (places * rows * (depth + columns) + depth * columns),
            transcendentals=0,
        ),
    )(table, *blocks, weight)


def plus(*blocks):
    return sum(block.astype(jnp.float32) for block in blocks).astype(jnp.bfloat16)


def ring_order(count):
    return list(range(0, count, 2)) + list(range(count - 1, 0, -2))


class Ring:
    def __init__(self):
        count = lax.axis_size("mp")
        self.order = ring_order(count)
        where = jnp.asarray([self.order.index(device) for device in range(count)], jnp.int32)
        self.ahead = [(self.order[i], self.order[(i + 1) % count]) for i in range(count)]
        self.back = [(b, a) for a, b in self.ahead]
        self.count = count
        rows = lax.axis_size("row")
        pieces = count // rows
        slot_rows = jnp.arange(rows, dtype=jnp.int32)
        if rows == 4:
            slot_rows = slot_rows ^ lax.axis_index("row")
        owner = slot_rows[:, None] * pieces + jnp.arange(pieces, dtype=jnp.int32)
        self.relative = (where[owner.reshape(count)] - where[lax.axis_index("mp")]) % count

    def chain(self, partials, longer):
        n, h = self.count, self.count // 2
        hops = (h, h - 1) if longer else (h - 1, h)
        ahead = back = None
        for k in range(h):
            if k < hops[0]:
                own = partials[hops[0] - k]
                ahead = own if ahead is None else plus(own, ahead)
                ahead = lax.ppermute(ahead, "mp", self.ahead)
            if k < hops[1]:
                own = partials[n - hops[1] + k]
                back = own if back is None else plus(own, back)
                back = lax.ppermute(back, "mp", self.back)
        return plus(partials[0], ahead, back)


def place_rows(new_kv, accepted, dest, beams_here, drafts):
    columns = new_kv.shape[1]
    width = drafts * columns
    fresh_rows = new_kv.reshape(beams_here, drafts, columns)
    order = jnp.arange(drafts, dtype=jnp.int32)
    kept_mask = order[None, :] < accepted[:, None]
    kept_rows = jnp.where(kept_mask[..., None], fresh_rows, jnp.zeros_like(fresh_rows))
    labels = jnp.stack([dest // beams_here, dest % beams_here], 1).astype(jnp.bfloat16)
    labels = jnp.pad(labels, ((0, 0), (0, 126)))
    sent = jnp.concatenate([kept_rows.reshape(beams_here, width), labels], 1)
    all_rows = jnp.concatenate(gather_rows(sent), 0)
    places = all_rows[:, width : width + 2].astype(jnp.int32)
    all_dest = places[:, 0] * beams_here + places[:, 1]
    slot = lax.axis_index("row") * beams_here + jnp.arange(beams_here, dtype=jnp.int32)
    placer = (all_dest[None, :] == slot[:, None]).astype(jnp.bfloat16)
    next_kv = jnp.dot(placer, all_rows[:, :width], preferred_element_type=jnp.float32)
    return next_kv.astype(jnp.bfloat16).reshape(beams_here, drafts, columns)


def after(value, *others):
    return lax.optimization_barrier((value, *others))[0]


def shards(queries, new_kv, cache_keys, cache_values, cache_lens, accepted, dest, out_weight):
    beams_here, halves_held, half_length, head_size = cache_keys.shape
    drafts = queries.shape[0] // beams_here
    depth = queries.shape[1]
    pieces = lax.axis_size("mp") // lax.axis_size("row")
    per_piece = beams_here // pieces
    ring = Ring()
    if halves_held == 1:
        whole = half_attention(queries, new_kv, cache_keys, cache_values, cache_lens)
        whole = whole.reshape(pieces, per_piece * drafts, depth)
    def attention(first, count, before):
        if halves_held == 1:
            return whole[:, first * drafts : (first + count) * drafts]
        q = after(queries, before)
        return attend(q, cache_keys, cache_values, new_kv, cache_lens, first, count, pieces, drafts)

    def halves_of(blocks, before=None):
        parts = []
        for side in range(2):
            if before is not None:
                blocks = [after(blocks[0], before)] + list(blocks[1:])
            part = project(ring.relative, blocks, out_weight, side, 2, True)
            before = part[0]
            parts.append(part)
        return parts

    first = attention(0, early_beams, queries)
    if lax.axis_size("row") == 4:
        far = partner(first, "row", 1)
        near = partner(first, "row", 0)
        second = attention(early_beams, per_piece - early_beams, near)
        second_far = partner(second, "row", 1)
        second_near = partner(second, "row", 0)
        far = after(far, second_near)
        early = halves_of([first, near, far, partner(far, "row", 0)])
        second_far = after(second_far, early[1][0])
        gathered = [second, second_near, second_far, partner(second_far, "row", 0)]
    else:
        early = halves_of(gather_rows(first))
        gathered = gather_rows(attention(early_beams, per_piece - early_beams, first))
    early = [ring.chain(part, side == 0) for side, part in enumerate(early)]
    late = [ring.chain(part, side == 0) for side, part in enumerate(halves_of(gathered))]
    mixed = jnp.concatenate([jnp.concatenate(early, 1), jnp.concatenate(late, 1)], 0)
    moved = after(new_kv, gathered[-1])
    next_kv = place_rows(moved, accepted, dest, beams_here, drafts)
    return (mixed, next_kv)


def solution(mesh):
    placed = (
        P("row", "mp"),
        P("row", "mp"),
        P("row", "mp", None, None),
        P("row", "mp", None, None),
        P("row"),
        P("row"),
        P("row"),
        P("mp", "row"),
    )
    return jax.shard_map(
        shards,
        mesh=mesh,
        in_specs=placed,
        out_specs=(P("mp", "row"), P("row", None, "mp")),
        check_vma=False,
    )
```

```python
import functools

import jax
import jax.numpy as jnp
from jax import lax
from jax.experimental import pallas as pl
from jax.experimental.pallas import tpu as pltpu
from jax.sharding import PartitionSpec as P

masked_score = -1e30
vmem_bytes = 60 * 2**20
early_beams = 8
order_of_work = ("one", "product", "kept", "one", "product", "0", "one")


def partner(block, axis, bit):
    count = lax.axis_size(axis)
    route = []
    for low in range(count):
        high = low | 1 << bit
        if high != low and high < count:
            route += [(low, high), (high, low)]
    return lax.ppermute(block, axis, route)


def head_slice(values, start, count):
    return lax.dynamic_slice_in_dim(values, start, count, 3)


def attention_kernel(scale, first, count, drafts, group, ahead, lens, q, k, v, fresh, out,
                     q_raw, q_wide, f_wide, o_wide, k_held, v_held, order, q_sems, k_sems, v_sems):
    halves = out.shape[0]
    size = k.shape[2]
    span = k.shape[1]
    heads = q.shape[1] // size
    stride = k.shape[0] // halves
    block = 2 * size
    most = span // block
    beams = halves * count
    groups = beams // group
    low = first * drafts // 16 * 16
    shift = first * drafts - low
    taken = q_raw.shape[1]
    rows = heads * drafts

    def half_of(i):
        return sum((i >= h * count).astype(jnp.int32) for h in range(1, halves))

    def beam_of(i):
        return i + half_of(i) * (stride - count) + first

    def blocks_of(i):
        return sum((lens[beam_of(i)] + drafts > c * block).astype(jnp.int32) for c in range(1, most)) + 1

    def tally(i, totals):
        held = blocks_of(i)
        return tuple(total + (held <= c + 1).astype(jnp.int32) for c, total in enumerate(totals))

    def rank(i, starts):
        held = blocks_of(i)
        spot = starts[0]
        for c in range(1, most):
            spot = jnp.where(held == c + 1, starts[c], spot)
        order[spot] = i
        return tuple(start + (held == c + 1).astype(jnp.int32) for c, start in enumerate(starts))

    def copies(g, c):
        part = pl.ds(0, c * block)
        for m in range(group):
            at = g * group + m
            beam = beam_of(order[at])
            yield pltpu.make_async_copy(k.at[beam, part], k_held.at[at, part], k_sems.at[at])
            yield pltpu.make_async_copy(v.at[beam, part], v_held.at[at, part], v_sems.at[at])

    def by_length(g, do):
        held = blocks_of(order[g * group + group - 1])
        for c in range(1, most + 1):
            pl.when(held == c)(functools.partial(do, g, c))

    def begin(g, c):
        for copy in copies(g, c):
            copy.start()

    def query_copy(h):
        start = h * stride * drafts + low
        return pltpu.make_async_copy(q.at[pl.ds(start, taken)], q_raw.at[h], q_sems.at[h])

    for h in range(halves):
        query_copy(h).start()
    totals = lax.fori_loop(0, beams, tally, (jnp.int32(0),) * most)
    lax.fori_loop(0, beams, rank, (jnp.int32(0),) + totals[:-1])
    ahead = min(ahead, groups)
    for g in range(ahead):
        by_length(g, begin)
    for side in range(2):
        f_wide[side, : fresh.shape[0]] = fresh[:, side * size : (side + 1) * size].astype(jnp.float32)
        f_wide[side, fresh.shape[0] :] = jnp.zeros((8, size), jnp.float32)
    for h in range(halves):
        query_copy(h).wait()
        q_wide[h] = q_raw[h].astype(jnp.float32).reshape(taken, heads, size)

    draft = lax.broadcasted_iota(jnp.int32, (2 * rows, 1), 0) % rows // heads
    upper = lax.broadcasted_iota(jnp.int32, (2 * rows, 1), 0) < rows
    window = 32
    spot = lax.broadcasted_iota(jnp.int32, (window, 1), 0)
    contract = (((1,), (1,)), ((), ()))
    blank = jnp.zeros((rows, size), jnp.bfloat16)

    def attend_group(g, c):
        width = c * block
        for copy in copies(g, c):
            copy.wait()
        chosen = []
        for m in range(group):
            i = g * group + m
            picked = order[i]
            half, beam = half_of(picked), beam_of(picked)
            length = lens[beam]
            at = jnp.minimum(lax.shift_left(lax.shift_right_logical(length, 4), 4), width - window)
            at = pl.multiple_of(at, 16)
            there = length - at
            inside = (spot >= there) & (spot < there + drafts)
            for side, held in enumerate((k_held, v_held)):
                new = f_wide[side, pl.ds(beam * drafts, 8), :]
                new = jnp.concatenate([new, jnp.zeros((window - 8, size), jnp.float32)], 0)
                new = pltpu.roll(new, there, 0).astype(jnp.bfloat16)
                old = held[i, pl.ds(at, window), :]
                held[i, pl.ds(at, window), :] = jnp.where(inside, new, old)
            chosen.append((i, length, half, (picked - half * count) * drafts))
        spots = lax.broadcasted_iota(jnp.int32, (1, width), 1)
        scores, limits = [], []
        for one, two in zip(chosen[::2], chosen[1::2]):
            qs = [
                q_wide[half, pl.ds(shift + row, drafts)].reshape(rows, size).astype(jnp.bfloat16)
                for _, _, half, row in (one, two)
            ]
            left = jnp.concatenate(
                [jnp.concatenate([qs[0], blank], 1), jnp.concatenate([blank, qs[1]], 1)], 0
            )
            keys = jnp.concatenate([k_held[one[0], :width], k_held[two[0], :width]], 1)
            scores.append(lax.dot_general(left, keys, contract, preferred_element_type=jnp.float32))
            limits.append(jnp.where(upper, one[1], two[1]) + draft)
        weights = []
        for s, limit in zip(scores, limits):
            s = jnp.where(spots <= limit, s, masked_score)
            top = jnp.max(s, 1, keepdims=True)
            w = jnp.exp((s - top) * scale).astype(jnp.bfloat16)
            weights.append((w, 1.0 / jnp.sum(w.astype(jnp.float32), 1, keepdims=True)))
        totals = []
        for (w, share), one, two in zip(weights, chosen[::2], chosen[1::2]):
            values = jnp.concatenate([v_held[one[0], :width], v_held[two[0], :width]], 1)
            totals.append(jnp.dot(w, values, preferred_element_type=jnp.float32) * share)
        for total, one, two in zip(totals, chosen[::2], chosen[1::2]):
            for m, (_, _, half, row) in enumerate((one, two)):
                part = total[m * rows : (m + 1) * rows, m * size : (m + 1) * size]
                o_wide[half, pl.ds(row, drafts)] = part.reshape(drafts, heads, size)

    def step(g, carry):
        @pl.when(g + ahead < groups)
        def _():
            by_length(jnp.minimum(g + ahead, groups - 1), begin)

        by_length(g, attend_group)
        return carry

    lax.fori_loop(0, groups, step, 0)
    for h in range(halves):
        out[h] = o_wide[h].reshape(out.shape[1], out.shape[2]).astype(out.dtype)


def attend(q, k, v, fresh, lens, first, count, halves, drafts, group=8, ahead=6):
    beams, size = k.shape[0], k.shape[3]
    span = k.shape[1] * k.shape[2]
    columns = q.shape[1]
    heads = columns // size
    stride = beams // halves
    taken = (first + count) * drafts - first * drafts // 16 * 16
    taken = (taken + 15) // 16 * 16
    chosen = halves * count
    full = pl.BlockSpec(memory_space=pltpu.VMEM)
    outside = pl.BlockSpec(memory_space=pl.ANY)
    return pl.pallas_call(
        functools.partial(attention_kernel, size**-0.5, first, count, drafts, group, ahead),
        out_shape=jax.ShapeDtypeStruct((halves, count * drafts, columns), jnp.bfloat16),
        in_specs=[pl.BlockSpec(memory_space=pltpu.SMEM), outside, outside, outside, full],
        out_specs=full,
        scratch_shapes=[
            pltpu.VMEM((halves, taken, columns), jnp.bfloat16),
            pltpu.VMEM((halves, taken, heads, size), jnp.float32),
            pltpu.VMEM((2, fresh.shape[0] + 8, size), jnp.float32),
            pltpu.VMEM((halves, count * drafts, heads, size), jnp.float32),
            pltpu.VMEM((chosen, span, size), jnp.bfloat16),
            pltpu.VMEM((chosen, span, size), jnp.bfloat16),
            pltpu.SMEM((chosen,), jnp.int32),
            pltpu.SemaphoreType.DMA((halves,)),
            pltpu.SemaphoreType.DMA((chosen,)),
            pltpu.SemaphoreType.DMA((chosen,)),
        ],
        compiler_params=pltpu.CompilerParams(vmem_limit_bytes=vmem_bytes),
        cost_estimate=pl.CostEstimate(
            flops=4 * halves * count * drafts * columns * span,
            bytes_accessed=4 * halves * count * size * span,
            transcendentals=halves * count * drafts * heads * span,
        ),
    )(lens, q, k.reshape(beams, span, size), v.reshape(beams, span, size), fresh)


def half_attention(queries, new_kv, cache_keys, cache_values, cache_lens):
    beams_here, halves_held, half_length, head_size = cache_keys.shape
    drafts = queries.shape[0] // beams_here
    heads_owned = queries.shape[1] // head_size
    mp_place = lax.axis_index("mp")
    lower_side = mp_place % 2 == 0
    partner_queries, partner_fresh = partner((queries, new_kv), "mp", 0)
    group_queries = jnp.where(
        lower_side,
        jnp.concatenate([queries, partner_queries], 1),
        jnp.concatenate([partner_queries, queries], 1),
    )
    fresh_pair = jnp.where(
        lower_side,
        jnp.concatenate([new_kv, partner_fresh], 1),
        jnp.concatenate([partner_fresh, new_kv], 1),
    )
    group_heads = group_queries.shape[1] // head_size
    sides = (mp_place * halves_held + jnp.arange(halves_held, dtype=jnp.int32)) % 2
    query_block = group_queries.reshape(beams_here, drafts, group_heads, head_size)
    fresh_block = fresh_pair.reshape(beams_here, drafts, 2, head_size)
    fresh_keys = fresh_block[:, :, 0]
    fresh_values = fresh_block[:, :, 1]
    scale = head_size ** (-0.5)
    cache_scores = (
        jnp.einsum("btjd,bsid->bstji", query_block, cache_keys, preferred_element_type=jnp.float32)
        * scale
    )
    fresh_scores = (
        jnp.einsum("btjd,bud->btju", query_block, fresh_keys, preferred_element_type=jnp.float32)
        * scale
    )
    spots = sides[:, None] * half_length + jnp.arange(half_length, dtype=jnp.int32)[None, :]
    cache_valid = (spots[None] < cache_lens[:, None, None])[:, :, None, None, :]
    order = jnp.arange(drafts, dtype=jnp.int32)
    fresh_side = (cache_lens[:, None] + order[None, :]) // half_length
    causal = order[:, None] >= order[None, :]
    fresh_valid = (
        causal[None, None] & (fresh_side[:, None, None, :] == sides[None, :, None, None])
    )[:, :, :, None, :]
    cache_masked = jnp.where(cache_valid, cache_scores, masked_score)
    fresh_masked = jnp.where(fresh_valid, fresh_scores[:, None], masked_score)
    highest = jnp.maximum(jnp.max(cache_masked, -1), jnp.max(fresh_masked, -1))
    cache_weights = jnp.where(cache_valid, jnp.exp(cache_masked - highest[..., None]), 0.0).astype(
        jnp.bfloat16
    )
    fresh_weights = jnp.where(fresh_valid, jnp.exp(fresh_masked - highest[..., None]), 0.0).astype(
        jnp.bfloat16
    )
    partial_value = jnp.einsum(
        "bstji,bsid->bstjd", cache_weights, cache_values, preferred_element_type=jnp.float32
    )
    partial_value = partial_value + jnp.einsum(
        "bstju,bud->bstjd", fresh_weights, fresh_values, preferred_element_type=jnp.float32
    )
    weight_mass = jnp.sum(cache_weights.astype(jnp.float32), -1) + jnp.sum(
        fresh_weights.astype(jnp.float32), -1
    )
    own_start = jnp.where(lower_side, 0, heads_owned).astype(jnp.int32)
    other_start = (heads_owned - own_start).astype(jnp.int32)
    got_partial, got_highest, got_mass = partner(
        (
            head_slice(partial_value, other_start, heads_owned),
            head_slice(highest, other_start, heads_owned),
            head_slice(weight_mass, other_start, heads_owned),
        ),
        "mp",
        0,
    )
    both_partial = jnp.concatenate(
        [head_slice(partial_value, own_start, heads_owned), got_partial], 1
    )
    both_highest = jnp.concatenate([head_slice(highest, own_start, heads_owned), got_highest], 1)
    both_mass = jnp.concatenate([head_slice(weight_mass, own_start, heads_owned), got_mass], 1)
    summit = jnp.max(both_highest, 1)
    factor = jnp.exp(both_highest - summit[:, None])
    numer = jnp.sum(factor[..., None] * both_partial, 1)
    denom = jnp.sum(factor * both_mass, 1)
    return (
        (numer / denom[..., None])
        .astype(jnp.bfloat16)
        .reshape(beams_here * drafts, heads_owned * head_size)
    )


def gather_rows(block):
    count = lax.axis_size("row")
    if count != 4:
        return [lax.all_gather(block, "row", axis=0, tiled=False)[j] for j in range(count)]
    near = partner(block, "row", 0)
    far = partner(block, "row", 1)
    return [block, near, far, partner(far, "row", 0)]


def project_kernel(gathered, pieces, half, table, *refs):
    blocks, weight = refs[:gathered], refs[gathered]
    out, held = refs[gathered + 1 : -1], refs[-1]
    rows = blocks[0].shape[1]
    places = held.shape[0] // rows
    pairs = half - 1
    ahead, back = out[:pairs], out[pairs : 2 * pairs]
    ahead_last, back_last, own_left, own_right = out[2 * pairs :]
    phase = pl.program_id(0) // (pl.num_programs(0) // 2)

    @pl.when(pl.program_id(0) == 0)
    def _():
        for at, block in enumerate(blocks):
            for piece in range(pieces):
                place = table[at * pieces + piece]
                for spot in range(places):

                    @pl.when(place == spot)
                    def _():
                        held[pl.ds(spot * rows, rows)] = block[piece]

    total = jnp.dot(held[...], weight[...], preferred_element_type=jnp.float32)
    total = total.astype(jnp.bfloat16)

    def of(place):
        place = place % places
        return total[place * rows : (place + 1) * rows]

    @pl.when(phase == 0)
    def _():
        for k in range(pairs):
            ahead[k][0] = of(half - k)
            back[k][0] = of(k + 1 - half)
        ahead_last[...] = of(1)
        own_left[...] = of(0)

    @pl.when(phase == 1)
    def _():
        for k in range(pairs):
            ahead[k][0] = of(half - 1 - k)
            back[k][0] = of(k - half)
        back_last[...] = of(-1)
        own_right[...] = of(0)


def project(table, blocks, weight):
    pieces, rows, depth = blocks[0].shape
    places = pieces * len(blocks)
    half = places // 2
    columns = weight.shape[1] // 2
    tile = min(1024, columns)
    tiles = columns // tile
    pair = jax.ShapeDtypeStruct((2, rows, columns), jnp.bfloat16)
    single = jax.ShapeDtypeStruct((rows, columns), jnp.bfloat16)
    ahead = pl.BlockSpec((1, rows, tile), lambda n, t: (n // tiles, 0, n % tiles))
    back = pl.BlockSpec((1, rows, tile), lambda n, t: (1 - n // tiles, 0, n % tiles))
    first = pl.BlockSpec((rows, tile), lambda n, t: (0, jnp.minimum(n, tiles - 1)))
    second = pl.BlockSpec((rows, tile), lambda n, t: (0, jnp.maximum(n - tiles, 0)))
    out = pl.pallas_call(
        functools.partial(project_kernel, len(blocks), pieces, half),
        out_shape=[pair] * (2 * half - 2) + [single] * 4,
        grid_spec=pltpu.PrefetchScalarGridSpec(
            num_scalar_prefetch=1,
            grid=(2 * tiles,),
            in_specs=[pl.BlockSpec((pieces, rows, depth), lambda n, t: (0, 0, 0))] * len(blocks)
            + [pl.BlockSpec((depth, tile), lambda n, t: (0, n))],
            out_specs=[ahead] * (half - 1) + [back] * (half - 1) + [first, second, first, second],
            scratch_shapes=[pltpu.VMEM((places * rows, depth), jnp.bfloat16)],
        ),
        compiler_params=pltpu.CompilerParams(vmem_limit_bytes=vmem_bytes),
        cost_estimate=pl.CostEstimate(
            flops=4 * places * rows * depth * columns,
            bytes_accessed=4 * (places * rows * (depth + columns) + depth * columns),
            transcendentals=0,
        ),
    )(table, *blocks, weight)
    steps = [list(step) for step in zip(out[: half - 1], out[half - 1 : 2 * half - 2])]
    return steps + [list(out[-4:-2])], list(out[-2:])


def project_side_kernel(gathered, pieces, table, *refs):
    blocks, weight = refs[:gathered], refs[gathered]
    out, held = refs[gathered + 1 : -1], refs[-1]
    rows = blocks[0].shape[1]
    places = held.shape[0] // rows

    @pl.when(pl.program_id(0) == 0)
    def _():
        for at, block in enumerate(blocks):
            for piece in range(pieces):
                place = table[at * pieces + piece]
                for spot in range(places):

                    @pl.when(place == spot)
                    def _():
                        held[pl.ds(spot * rows, rows)] = block[piece]

    total = jnp.dot(held[...], weight[...], preferred_element_type=jnp.float32)
    total = total.astype(jnp.bfloat16)
    for spot in range(places):
        out[spot][...] = total[spot * rows : (spot + 1) * rows]


def project_side(table, blocks, weight, side):
    pieces, rows, depth = blocks[0].shape
    columns = weight.shape[1] // 2
    tile = min(512, columns)
    tiles = columns // tile
    places = pieces * len(blocks)
    return pl.pallas_call(
        functools.partial(project_side_kernel, len(blocks), pieces),
        out_shape=[jax.ShapeDtypeStruct((rows, columns), jnp.bfloat16)] * places,
        grid_spec=pltpu.PrefetchScalarGridSpec(
            num_scalar_prefetch=1,
            grid=(tiles,),
            in_specs=[pl.BlockSpec((pieces, rows, depth), lambda n, t: (0, 0, 0))] * len(blocks)
            + [pl.BlockSpec((depth, tile), lambda n, t: (0, n + side * tiles))],
            out_specs=[pl.BlockSpec((rows, tile), lambda n, t: (0, n))] * places,
            scratch_shapes=[pltpu.VMEM((places * rows, depth), jnp.bfloat16)],
        ),
        compiler_params=pltpu.CompilerParams(vmem_limit_bytes=vmem_bytes),
        cost_estimate=pl.CostEstimate(
            flops=2 * places * rows * depth * columns,
            bytes_accessed=2 * (places * rows * (depth + columns) + depth * columns),
            transcendentals=0,
        ),
    )(table, *blocks, weight)


def plus(*blocks):
    return sum(block.astype(jnp.float32) for block in blocks).astype(jnp.bfloat16)


def ring_order(count):
    return list(range(0, count, 2)) + list(range(count - 1, 0, -2))


class Ring:
    def __init__(self):
        count = lax.axis_size("mp")
        order = ring_order(count)
        self.ahead = [(order[i], order[(i + 1) % count]) for i in range(count)]
        self.back = [(b, a) for a, b in self.ahead]
        self.count = count
        rows = lax.axis_size("row")
        slot = jnp.arange(count, dtype=jnp.int32)
        pieces = count // rows
        slot_row = slot // pieces
        if rows == 4:
            slot_row = slot_row ^ lax.axis_index("row")
        owner = slot_row * pieces + slot % pieces
        self.relative = (self.place(owner) - self.place(lax.axis_index("mp"))) % count

    def place(self, device):
        return jnp.where(device % 2 == 0, device // 2, self.count - 1 - device // 2)


class Chain:
    def __init__(self, ring, partials):
        self.ring = ring
        self.partials, self.own = partials
        self.arrived = None
        self.step = 0

    def advance(self, before=()):
        sent = self.partials[self.step]
        if self.arrived is not None:
            arrived = lax.optimization_barrier((*self.arrived, *before))[:2]
            if self.step == len(self.partials) - 1:
                self.own = [plus(self.own[0], arrived[1][1]), plus(self.own[1], arrived[0][1])]
                arrived = [got[0] for got in arrived]
            sent = [plus(own, got) for own, got in zip(sent, arrived)]
        routes = (self.ring.ahead, self.ring.back)
        self.arrived = [lax.ppermute(block, "mp", route) for block, route in zip(sent, routes)]
        self.step += 1
        return sent

    def finish(self, before):
        arrived = lax.optimization_barrier((*self.arrived, *before))[:2]
        return jnp.concatenate([plus(own, got) for own, got in zip(self.own, arrived)], 1)


class SideChain:
    def __init__(self, ring, partials, longer):
        half = ring.count // 2
        self.ring = ring
        self.partials = partials
        self.hops = (half, half - 1) if longer else (half - 1, half)
        self.arrived = []
        self.step = 0

    def advance(self, before=()):
        k, n = self.step, self.ring.count
        places = (self.hops[0] - k, n - self.hops[1] + k)
        arrived = list(self.arrived)
        if arrived:
            arrived = lax.optimization_barrier((*arrived, *before))[:2]
        sent, self.arrived = [], []
        for way, route in enumerate((self.ring.ahead, self.ring.back)):
            if k < self.hops[way]:
                own = self.partials[places[way]]
                own = plus(own, arrived[way]) if arrived else own
                sent.append(own)
                self.arrived.append(lax.ppermute(own, "mp", route))
            else:
                self.arrived.append(arrived[way])
        self.step += 1
        return sent

    def finish(self, before):
        arrived = lax.optimization_barrier((*self.arrived, *before))[:2]
        return plus(self.partials[0], *arrived)


def kept_rows(new_kv, accepted, dest, beams_here, drafts):
    columns = new_kv.shape[1]
    fresh_rows = new_kv.reshape(beams_here, drafts, columns)
    order = jnp.arange(drafts, dtype=jnp.int32)
    kept_mask = order[None, :] < accepted[:, None]
    kept = jnp.where(kept_mask[..., None], fresh_rows, jnp.zeros_like(fresh_rows))
    labels = jnp.stack([dest // beams_here, dest % beams_here], 1).astype(jnp.bfloat16)
    labels = jnp.pad(labels, ((0, 0), (0, 126)))
    return jnp.concatenate([kept.reshape(beams_here, drafts * columns), labels], 1)


def place_rows(gathered, beams_here, drafts, columns):
    width = drafts * columns
    all_rows = jnp.concatenate(gathered, 0)
    places = all_rows[:, width : width + 2].astype(jnp.int32)
    all_dest = places[:, 0] * beams_here + places[:, 1]
    slot = lax.axis_index("row") * beams_here + jnp.arange(beams_here, dtype=jnp.int32)
    placer = (all_dest[None, :] == slot[:, None]).astype(jnp.bfloat16)
    next_kv = jnp.dot(placer, all_rows[:, :width], preferred_element_type=jnp.float32)
    return next_kv.astype(jnp.bfloat16).reshape(beams_here, drafts, columns)


def after(value, *others):
    return lax.optimization_barrier((value, *others))[0]


def shards(queries, new_kv, cache_keys, cache_values, cache_lens, accepted, dest, out_weight):
    beams_here, halves_held, half_length, head_size = cache_keys.shape
    drafts = queries.shape[0] // beams_here
    depth = queries.shape[1]
    pieces = lax.axis_size("mp") // lax.axis_size("row")
    per_piece = beams_here // pieces
    ring = Ring()
    if halves_held == 1:
        whole = half_attention(queries, new_kv, cache_keys, cache_values, cache_lens)
        whole = whole.reshape(pieces, per_piece * drafts, depth)
    def attention(first, count, before):
        if halves_held == 1:
            return whole[:, first * drafts : (first + count) * drafts]
        q = after(queries, before)
        return attend(q, cache_keys, cache_values, new_kv, cache_lens, first, count, pieces, drafts)

    def chain_of(blocks, before=()):
        blocks = [after(blocks[0], *before)] + list(blocks[1:]) if before else blocks
        return Chain(ring, project(ring.relative, blocks, out_weight))

    by_chip = lax.axis_size("row") == 4
    first = attention(0, early_beams, queries)
    if by_chip:
        far = partner(first, "row", 1)
        near = partner(first, "row", 0)
        second = attention(early_beams, per_piece - early_beams, first)
        second_far = partner(second, "row", 1)
        second_near = partner(second, "row", 0)
        far = after(far, second)
        early = [first, near, far, partner(far, "row", 0)]
    else:
        early = gather_rows(first)
    chain_one = chain_of(early)
    sent = chain_one.advance()
    kept = kept_rows(after(new_kv, *sent), accepted, dest, beams_here, drafts)
    if by_chip:
        second_far = after(second_far, *sent)
        late = [second, second_near, second_far, partner(second_far, "row", 0)]
        kept_far = partner(kept, "row", 1)
        kept_near = partner(kept, "row", 0)
    else:
        late = gather_rows(attention(early_beams, per_piece - early_beams, first))
        kept = gather_rows(kept)
    half = ring.count // 2
    sides = []
    for word in order_of_work:
        if word == "one":
            sent = chain_one.advance(sent)
        elif word == "product":
            blocks = [after(late[0], *sent)] + late[1:]
            partials = project_side(ring.relative, blocks, out_weight, len(sides))
            sides.append(SideChain(ring, partials, not sides))
            sides[-1].advance()
            sent = partials[:1]
        elif word == "kept" and by_chip:
            kept_far, kept_near = lax.optimization_barrier((kept_far, kept_near, *sent))[:2]
            sent = (*sent, kept_far, kept_near)
            kept = [kept, kept_near, kept_far, partner(kept_far, "row", 0)]
        elif word in ("0", "1"):
            sent = sides[int(word)].advance(sent)
    for step in range(chain_one.step, half):
        sent = chain_one.advance(sent)
    for step in range(1, half):
        for side in range(2):
            if sides[side].step == step:
                sent = sides[side].advance(sent)
    kept[-1] = after(kept[-1], *sent)
    next_kv = place_rows(kept, beams_here, drafts, new_kv.shape[1])
    done = [chain_one.finish(sent)]
    done.append(sides[0].finish(done[:1]))
    done.append(sides[1].finish(done[1:]))
    mixed = jnp.concatenate([done[0], jnp.concatenate(done[1:], 1)], 0)
    return (mixed, next_kv)


def solution(mesh):
    placed = (
        P("row", "mp"),
        P("row", "mp"),
        P("row", "mp", None, None),
        P("row", "mp", None, None),
        P("row"),
        P("row"),
        P("row"),
        P("mp", "row"),
    )
    return jax.shard_map(
        shards,
        mesh=mesh,
        in_specs=placed,
        out_specs=(P("mp", "row"), P("row", None, "mp")),
        check_vma=False,
    )
```

```python
import functools

import jax
import jax.numpy as jnp
from jax import lax
from jax.experimental import pallas as pl
from jax.experimental.pallas import tpu as pltpu
from jax.sharding import PartitionSpec as P

masked_score = -1e30
vmem_bytes = 60 * 2**20
early_beams = 8
order_of_work = ("one", "product", "kept", "one", "product", "0", "one")


def partner(block, axis, bit):
    count = lax.axis_size(axis)
    route = []
    for low in range(count):
        high = low | 1 << bit
        if high != low and high < count:
            route += [(low, high), (high, low)]
    return lax.ppermute(block, axis, route)


def head_slice(values, start, count):
    return lax.dynamic_slice_in_dim(values, start, count, 3)


def attention_kernel(scale, first, count, drafts, group, ahead, lens, q, k, v, fresh, out,
                     q_raw, q_wide, f_raw, f_wide, o_wide, k_held, v_held, order, f_sem, q_sems, k_sems, v_sems):
    halves = out.shape[0]
    size = k.shape[2]
    span = k.shape[1]
    heads = q.shape[1] // size
    stride = k.shape[0] // halves
    block = 2 * size
    most = span // block
    beams = halves * count
    groups = beams // group
    low = first * drafts // 16 * 16
    shift = first * drafts - low
    taken = q_raw.shape[1]
    rows = heads * drafts

    def half_of(i):
        return sum((i >= h * count).astype(jnp.int32) for h in range(1, halves))

    def beam_of(i):
        return i + half_of(i) * (stride - count) + first

    def blocks_of(i):
        return sum((lens[beam_of(i)] + drafts > c * block).astype(jnp.int32) for c in range(1, most)) + 1

    def tally(i, totals):
        held = blocks_of(i)
        return tuple(total + (held <= c + 1).astype(jnp.int32) for c, total in enumerate(totals))

    def rank(i, starts):
        held = blocks_of(i)
        spot = starts[0]
        for c in range(1, most):
            spot = jnp.where(held == c + 1, starts[c], spot)
        order[spot] = i
        return tuple(start + (held == c + 1).astype(jnp.int32) for c, start in enumerate(starts))

    def copies(g, c):
        part = pl.ds(0, c * block)
        for m in range(group):
            at = g * group + m
            beam = beam_of(order[at])
            yield pltpu.make_async_copy(k.at[beam, part], k_held.at[at, part], k_sems.at[at])
            yield pltpu.make_async_copy(v.at[beam, part], v_held.at[at, part], v_sems.at[at])

    def by_length(g, do):
        held = blocks_of(order[g * group + group - 1])
        for c in range(1, most + 1):
            pl.when(held == c)(functools.partial(do, g, c))

    def begin(g, c):
        for copy in copies(g, c):
            copy.start()

    def query_copy(h):
        start = h * stride * drafts + low
        return pltpu.make_async_copy(q.at[pl.ds(start, taken)], q_raw.at[h], q_sems.at[h])

    fresh_copy = pltpu.make_async_copy(fresh, f_raw, f_sem)
    fresh_copy.start()
    for h in range(halves):
        query_copy(h).start()
    totals = lax.fori_loop(0, beams, tally, (jnp.int32(0),) * most, unroll=8)
    lax.fori_loop(0, beams, rank, (jnp.int32(0),) + totals[:-1], unroll=8)
    ahead = min(ahead, groups)
    for g in range(ahead):
        by_length(g, begin)
    fresh_copy.wait()
    for side in range(2):
        f_wide[side, : fresh.shape[0]] = f_raw[:, side * size : (side + 1) * size].astype(jnp.float32)
        f_wide[side, fresh.shape[0] :] = jnp.zeros((8, size), jnp.float32)
    for h in range(halves):
        query_copy(h).wait()
        q_wide[h] = q_raw[h].astype(jnp.float32).reshape(taken, heads, size)

    draft = lax.broadcasted_iota(jnp.int32, (2 * rows, 1), 0) % rows // heads
    upper = lax.broadcasted_iota(jnp.int32, (2 * rows, 1), 0) < rows
    window = 32
    spot = lax.broadcasted_iota(jnp.int32, (window, 1), 0)
    contract = (((1,), (1,)), ((), ()))
    blank = jnp.zeros((rows, size), jnp.bfloat16)

    def attend_group(g, c):
        width = c * block
        for copy in copies(g, c):
            copy.wait()
        chosen = []
        for m in range(group):
            i = g * group + m
            picked = order[i]
            half, beam = half_of(picked), beam_of(picked)
            length = lens[beam]
            at = jnp.minimum(lax.shift_left(lax.shift_right_logical(length, 4), 4), width - window)
            at = pl.multiple_of(at, 16)
            there = length - at
            inside = (spot >= there) & (spot < there + drafts)
            for side, held in enumerate((k_held, v_held)):
                new = f_wide[side, pl.ds(beam * drafts, 8), :]
                new = jnp.concatenate([new, jnp.zeros((window - 8, size), jnp.float32)], 0)
                new = pltpu.roll(new, there, 0).astype(jnp.bfloat16)
                old = held[i, pl.ds(at, window), :]
                held[i, pl.ds(at, window), :] = jnp.where(inside, new, old)
            chosen.append((i, length, half, (picked - half * count) * drafts))
        spots = lax.broadcasted_iota(jnp.int32, (1, width), 1)
        scores, limits = [], []
        for one, two in zip(chosen[::2], chosen[1::2]):
            qs = [
                q_wide[half, pl.ds(shift + row, drafts)].reshape(rows, size).astype(jnp.bfloat16)
                for _, _, half, row in (one, two)
            ]
            left = jnp.concatenate(
                [jnp.concatenate([qs[0], blank], 1), jnp.concatenate([blank, qs[1]], 1)], 0
            )
            keys = jnp.concatenate([k_held[one[0], :width], k_held[two[0], :width]], 1)
            scores.append(lax.dot_general(left, keys, contract, preferred_element_type=jnp.float32))
            limits.append(jnp.where(upper, one[1], two[1]) + draft)
        weights = []
        for s, limit in zip(scores, limits):
            s = jnp.where(spots <= limit, s, masked_score)
            top = jnp.max(s, 1, keepdims=True)
            w = jnp.exp((s - top) * scale).astype(jnp.bfloat16)
            weights.append((w, 1.0 / jnp.sum(w.astype(jnp.float32), 1, keepdims=True)))
        totals = []
        for (w, share), one, two in zip(weights, chosen[::2], chosen[1::2]):
            values = jnp.concatenate([v_held[one[0], :width], v_held[two[0], :width]], 1)
            totals.append(jnp.dot(w, values, preferred_element_type=jnp.float32) * share)
        for total, one, two in zip(totals, chosen[::2], chosen[1::2]):
            for m, (_, _, half, row) in enumerate((one, two)):
                part = total[m * rows : (m + 1) * rows, m * size : (m + 1) * size]
                o_wide[half, pl.ds(row, drafts)] = part.reshape(drafts, heads, size)

    def step(g, carry):
        @pl.when(g + ahead < groups)
        def _():
            by_length(jnp.minimum(g + ahead, groups - 1), begin)

        by_length(g, attend_group)
        return carry

    lax.fori_loop(0, groups, step, 0)
    for h in range(halves):
        out[h] = o_wide[h].reshape(out.shape[1], out.shape[2]).astype(out.dtype)


def attend(q, k, v, fresh, lens, first, count, halves, drafts, group=8, ahead=6):
    beams, size = k.shape[0], k.shape[3]
    span = k.shape[1] * k.shape[2]
    columns = q.shape[1]
    heads = columns // size
    stride = beams // halves
    taken = (first + count) * drafts - first * drafts // 16 * 16
    taken = (taken + 15) // 16 * 16
    chosen = halves * count
    group = group if count > 8 else 4
    full = pl.BlockSpec(memory_space=pltpu.VMEM)
    outside = pl.BlockSpec(memory_space=pl.ANY)
    return pl.pallas_call(
        functools.partial(attention_kernel, size**-0.5, first, count, drafts, group, ahead),
        out_shape=jax.ShapeDtypeStruct((halves, count * drafts, columns), jnp.bfloat16),
        in_specs=[pl.BlockSpec(memory_space=pltpu.SMEM), outside, outside, outside, outside],
        out_specs=full,
        scratch_shapes=[
            pltpu.VMEM((halves, taken, columns), jnp.bfloat16),
            pltpu.VMEM((halves, taken, heads, size), jnp.float32),
            pltpu.VMEM(fresh.shape, jnp.bfloat16),
            pltpu.VMEM((2, fresh.shape[0] + 8, size), jnp.float32),
            pltpu.VMEM((halves, count * drafts, heads, size), jnp.float32),
            pltpu.VMEM((chosen, span, size), jnp.bfloat16),
            pltpu.VMEM((chosen, span, size), jnp.bfloat16),
            pltpu.SMEM((chosen,), jnp.int32),
            pltpu.SemaphoreType.DMA,
            pltpu.SemaphoreType.DMA((halves,)),
            pltpu.SemaphoreType.DMA((chosen,)),
            pltpu.SemaphoreType.DMA((chosen,)),
        ],
        compiler_params=pltpu.CompilerParams(vmem_limit_bytes=vmem_bytes),
        cost_estimate=pl.CostEstimate(
            flops=4 * halves * count * drafts * columns * span,
            bytes_accessed=4 * halves * count * size * span,
            transcendentals=halves * count * drafts * heads * span,
        ),
    )(lens, q, k.reshape(beams, span, size), v.reshape(beams, span, size), fresh)


def half_attention(queries, new_kv, cache_keys, cache_values, cache_lens):
    beams_here, halves_held, half_length, head_size = cache_keys.shape
    drafts = queries.shape[0] // beams_here
    heads_owned = queries.shape[1] // head_size
    mp_place = lax.axis_index("mp")
    lower_side = mp_place % 2 == 0
    partner_queries, partner_fresh = partner((queries, new_kv), "mp", 0)
    group_queries = jnp.where(
        lower_side,
        jnp.concatenate([queries, partner_queries], 1),
        jnp.concatenate([partner_queries, queries], 1),
    )
    fresh_pair = jnp.where(
        lower_side,
        jnp.concatenate([new_kv, partner_fresh], 1),
        jnp.concatenate([partner_fresh, new_kv], 1),
    )
    group_heads = group_queries.shape[1] // head_size
    sides = (mp_place * halves_held + jnp.arange(halves_held, dtype=jnp.int32)) % 2
    query_block = group_queries.reshape(beams_here, drafts, group_heads, head_size)
    fresh_block = fresh_pair.reshape(beams_here, drafts, 2, head_size)
    fresh_keys = fresh_block[:, :, 0]
    fresh_values = fresh_block[:, :, 1]
    scale = head_size ** (-0.5)
    cache_scores = (
        jnp.einsum("btjd,bsid->bstji", query_block, cache_keys, preferred_element_type=jnp.float32)
        * scale
    )
    fresh_scores = (
        jnp.einsum("btjd,bud->btju", query_block, fresh_keys, preferred_element_type=jnp.float32)
        * scale
    )
    spots = sides[:, None] * half_length + jnp.arange(half_length, dtype=jnp.int32)[None, :]
    cache_valid = (spots[None] < cache_lens[:, None, None])[:, :, None, None, :]
    order = jnp.arange(drafts, dtype=jnp.int32)
    fresh_side = (cache_lens[:, None] + order[None, :]) // half_length
    causal = order[:, None] >= order[None, :]
    fresh_valid = (
        causal[None, None] & (fresh_side[:, None, None, :] == sides[None, :, None, None])
    )[:, :, :, None, :]
    cache_masked = jnp.where(cache_valid, cache_scores, masked_score)
    fresh_masked = jnp.where(fresh_valid, fresh_scores[:, None], masked_score)
    highest = jnp.maximum(jnp.max(cache_masked, -1), jnp.max(fresh_masked, -1))
    cache_weights = jnp.where(cache_valid, jnp.exp(cache_masked - highest[..., None]), 0.0).astype(
        jnp.bfloat16
    )
    fresh_weights = jnp.where(fresh_valid, jnp.exp(fresh_masked - highest[..., None]), 0.0).astype(
        jnp.bfloat16
    )
    partial_value = jnp.einsum(
        "bstji,bsid->bstjd", cache_weights, cache_values, preferred_element_type=jnp.float32
    )
    partial_value = partial_value + jnp.einsum(
        "bstju,bud->bstjd", fresh_weights, fresh_values, preferred_element_type=jnp.float32
    )
    weight_mass = jnp.sum(cache_weights.astype(jnp.float32), -1) + jnp.sum(
        fresh_weights.astype(jnp.float32), -1
    )
    own_start = jnp.where(lower_side, 0, heads_owned).astype(jnp.int32)
    other_start = (heads_owned - own_start).astype(jnp.int32)
    got_partial, got_highest, got_mass = partner(
        (
            head_slice(partial_value, other_start, heads_owned),
            head_slice(highest, other_start, heads_owned),
            head_slice(weight_mass, other_start, heads_owned),
        ),
        "mp",
        0,
    )
    both_partial = jnp.concatenate(
        [head_slice(partial_value, own_start, heads_owned), got_partial], 1
    )
    both_highest = jnp.concatenate([head_slice(highest, own_start, heads_owned), got_highest], 1)
    both_mass = jnp.concatenate([head_slice(weight_mass, own_start, heads_owned), got_mass], 1)
    summit = jnp.max(both_highest, 1)
    factor = jnp.exp(both_highest - summit[:, None])
    numer = jnp.sum(factor[..., None] * both_partial, 1)
    denom = jnp.sum(factor * both_mass, 1)
    return (
        (numer / denom[..., None])
        .astype(jnp.bfloat16)
        .reshape(beams_here * drafts, heads_owned * head_size)
    )


def gather_rows(block):
    count = lax.axis_size("row")
    if count != 4:
        return [lax.all_gather(block, "row", axis=0, tiled=False)[j] for j in range(count)]
    near = partner(block, "row", 0)
    far = partner(block, "row", 1)
    return [block, near, far, partner(far, "row", 0)]


def project_kernel(gathered, pieces, half, table, *refs):
    blocks, weight = refs[:gathered], refs[gathered]
    out, held = refs[gathered + 1 : -1], refs[-1]
    rows = blocks[0].shape[1]
    places = held.shape[0] // rows
    pairs = half - 1
    ahead, back = out[:pairs], out[pairs : 2 * pairs]
    ahead_last, back_last, own_left, own_right = out[2 * pairs :]
    phase = pl.program_id(0) // (pl.num_programs(0) // 2)

    @pl.when(pl.program_id(0) == 0)
    def _():
        for at, block in enumerate(blocks):
            for piece in range(pieces):
                place = table[at * pieces + piece]
                for spot in range(places):

                    @pl.when(place == spot)
                    def _():
                        held[pl.ds(spot * rows, rows)] = block[piece]

    total = jnp.dot(held[...], weight[...], preferred_element_type=jnp.float32)
    total = total.astype(jnp.bfloat16)

    def of(place):
        place = place % places
        return total[place * rows : (place + 1) * rows]

    @pl.when(phase == 0)
    def _():
        for k in range(pairs):
            ahead[k][0] = of(half - k)
            back[k][0] = of(k + 1 - half)
        ahead_last[...] = of(1)
        own_left[...] = of(0)

    @pl.when(phase == 1)
    def _():
        for k in range(pairs):
            ahead[k][0] = of(half - 1 - k)
            back[k][0] = of(k - half)
        back_last[...] = of(-1)
        own_right[...] = of(0)


def project(table, blocks, weight):
    pieces, rows, depth = blocks[0].shape
    places = pieces * len(blocks)
    half = places // 2
    columns = weight.shape[1] // 2
    tile = min(1024, columns)
    tiles = columns // tile
    pair = jax.ShapeDtypeStruct((2, rows, columns), jnp.bfloat16)
    single = jax.ShapeDtypeStruct((rows, columns), jnp.bfloat16)
    ahead = pl.BlockSpec((1, rows, tile), lambda n, t: (n // tiles, 0, n % tiles))
    back = pl.BlockSpec((1, rows, tile), lambda n, t: (1 - n // tiles, 0, n % tiles))
    first = pl.BlockSpec((rows, tile), lambda n, t: (0, jnp.minimum(n, tiles - 1)))
    second = pl.BlockSpec((rows, tile), lambda n, t: (0, jnp.maximum(n - tiles, 0)))
    out = pl.pallas_call(
        functools.partial(project_kernel, len(blocks), pieces, half),
        out_shape=[pair] * (2 * half - 2) + [single] * 4,
        grid_spec=pltpu.PrefetchScalarGridSpec(
            num_scalar_prefetch=1,
            grid=(2 * tiles,),
            in_specs=[pl.BlockSpec((pieces, rows, depth), lambda n, t: (0, 0, 0))] * len(blocks)
            + [pl.BlockSpec((depth, tile), lambda n, t: (0, n))],
            out_specs=[ahead] * (half - 1) + [back] * (half - 1) + [first, second, first, second],
            scratch_shapes=[pltpu.VMEM((places * rows, depth), jnp.bfloat16)],
        ),
        compiler_params=pltpu.CompilerParams(vmem_limit_bytes=vmem_bytes),
        cost_estimate=pl.CostEstimate(
            flops=4 * places * rows * depth * columns,
            bytes_accessed=4 * (places * rows * (depth + columns) + depth * columns),
            transcendentals=0,
        ),
    )(table, *blocks, weight)
    steps = [list(step) for step in zip(out[: half - 1], out[half - 1 : 2 * half - 2])]
    return steps + [list(out[-4:-2])], list(out[-2:])


def project_side_kernel(gathered, pieces, table, *refs):
    blocks, weight = refs[:gathered], refs[gathered]
    out, held = refs[gathered + 1 : -1], refs[-1]
    rows = blocks[0].shape[1]
    places = held.shape[0] // rows

    @pl.when(pl.program_id(0) == 0)
    def _():
        for at, block in enumerate(blocks):
            for piece in range(pieces):
                place = table[at * pieces + piece]
                for spot in range(places):

                    @pl.when(place == spot)
                    def _():
                        held[pl.ds(spot * rows, rows)] = block[piece]

    total = jnp.dot(held[...], weight[...], preferred_element_type=jnp.float32)
    total = total.astype(jnp.bfloat16)
    for spot in range(places):
        out[spot][...] = total[spot * rows : (spot + 1) * rows]


def project_side(table, blocks, weight, side):
    pieces, rows, depth = blocks[0].shape
    columns = weight.shape[1] // 2
    tile = min(512, columns)
    tiles = columns // tile
    places = pieces * len(blocks)
    return pl.pallas_call(
        functools.partial(project_side_kernel, len(blocks), pieces),
        out_shape=[jax.ShapeDtypeStruct((rows, columns), jnp.bfloat16)] * places,
        grid_spec=pltpu.PrefetchScalarGridSpec(
            num_scalar_prefetch=1,
            grid=(tiles,),
            in_specs=[pl.BlockSpec((pieces, rows, depth), lambda n, t: (0, 0, 0))] * len(blocks)
            + [pl.BlockSpec((depth, tile), lambda n, t: (0, n + side * tiles))],
            out_specs=[pl.BlockSpec((rows, tile), lambda n, t: (0, n))] * places,
            scratch_shapes=[pltpu.VMEM((places * rows, depth), jnp.bfloat16)],
        ),
        compiler_params=pltpu.CompilerParams(vmem_limit_bytes=vmem_bytes),
        cost_estimate=pl.CostEstimate(
            flops=2 * places * rows * depth * columns,
            bytes_accessed=2 * (places * rows * (depth + columns) + depth * columns),
            transcendentals=0,
        ),
    )(table, *blocks, weight)


def plus(*blocks):
    return sum(block.astype(jnp.float32) for block in blocks).astype(jnp.bfloat16)


def ring_order(count):
    return list(range(0, count, 2)) + list(range(count - 1, 0, -2))


class Ring:
    def __init__(self):
        count = lax.axis_size("mp")
        order = ring_order(count)
        self.ahead = [(order[i], order[(i + 1) % count]) for i in range(count)]
        self.back = [(b, a) for a, b in self.ahead]
        self.count = count
        rows = lax.axis_size("row")
        slot = jnp.arange(count, dtype=jnp.int32)
        pieces = count // rows
        slot_row = slot // pieces
        if rows == 4:
            slot_row = slot_row ^ lax.axis_index("row")
        owner = slot_row * pieces + slot % pieces
        self.relative = (self.place(owner) - self.place(lax.axis_index("mp"))) % count

    def place(self, device):
        return jnp.where(device % 2 == 0, device // 2, self.count - 1 - device // 2)


class Chain:
    def __init__(self, ring, partials):
        self.ring = ring
        self.partials, self.own = partials
        self.arrived = None
        self.step = 0

    def advance(self, before=()):
        sent = self.partials[self.step]
        if self.arrived is not None:
            arrived = lax.optimization_barrier((*self.arrived, *before))[:2]
            if self.step == len(self.partials) - 1:
                self.own = [plus(self.own[0], arrived[1][1]), plus(self.own[1], arrived[0][1])]
                arrived = [got[0] for got in arrived]
            sent = [plus(own, got) for own, got in zip(sent, arrived)]
        routes = (self.ring.ahead, self.ring.back)
        self.arrived = [lax.ppermute(block, "mp", route) for block, route in zip(sent, routes)]
        self.step += 1
        return sent

    def finish(self, before):
        arrived = lax.optimization_barrier((*self.arrived, *before))[:2]
        return jnp.concatenate([plus(own, got) for own, got in zip(self.own, arrived)], 1)


class SideChain:
    def __init__(self, ring, partials, longer):
        half = ring.count // 2
        self.ring = ring
        self.partials = partials
        self.hops = (half, half - 1) if longer else (half - 1, half)
        self.arrived = []
        self.step = 0

    def advance(self, before=()):
        k, n = self.step, self.ring.count
        places = (self.hops[0] - k, n - self.hops[1] + k)
        arrived = list(self.arrived)
        if arrived:
            arrived = lax.optimization_barrier((*arrived, *before))[:2]
        sent, self.arrived = [], []
        for way, route in enumerate((self.ring.ahead, self.ring.back)):
            if k < self.hops[way]:
                own = self.partials[places[way]]
                own = plus(own, arrived[way]) if arrived else own
                sent.append(own)
                self.arrived.append(lax.ppermute(own, "mp", route))
            else:
                self.arrived.append(arrived[way])
        self.step += 1
        return sent

    def finish(self, before):
        arrived = lax.optimization_barrier((*self.arrived, *before))[:2]
        return plus(self.partials[0], *arrived)


def kept_rows(new_kv, accepted, dest, beams_here, drafts):
    columns = new_kv.shape[1]
    fresh_rows = new_kv.reshape(beams_here, drafts, columns)
    order = jnp.arange(drafts, dtype=jnp.int32)
    kept_mask = order[None, :] < accepted[:, None]
    kept = jnp.where(kept_mask[..., None], fresh_rows, jnp.zeros_like(fresh_rows))
    labels = jnp.stack([dest // beams_here, dest % beams_here], 1).astype(jnp.bfloat16)
    labels = jnp.pad(labels, ((0, 0), (0, 126)))
    return jnp.concatenate([kept.reshape(beams_here, drafts * columns), labels], 1)


def place_rows(gathered, beams_here, drafts, columns):
    width = drafts * columns
    all_rows = jnp.concatenate(gathered, 0)
    places = all_rows[:, width : width + 2].astype(jnp.int32)
    all_dest = places[:, 0] * beams_here + places[:, 1]
    slot = lax.axis_index("row") * beams_here + jnp.arange(beams_here, dtype=jnp.int32)
    placer = (all_dest[None, :] == slot[:, None]).astype(jnp.bfloat16)
    next_kv = jnp.dot(placer, all_rows[:, :width], preferred_element_type=jnp.float32)
    return next_kv.astype(jnp.bfloat16).reshape(beams_here, drafts, columns)


def after(value, *others):
    return lax.optimization_barrier((value, *others))[0]


def shards(queries, new_kv, cache_keys, cache_values, cache_lens, accepted, dest, out_weight):
    beams_here, halves_held, half_length, head_size = cache_keys.shape
    drafts = queries.shape[0] // beams_here
    depth = queries.shape[1]
    pieces = lax.axis_size("mp") // lax.axis_size("row")
    per_piece = beams_here // pieces
    ring = Ring()
    if halves_held == 1:
        whole = half_attention(queries, new_kv, cache_keys, cache_values, cache_lens)
        whole = whole.reshape(pieces, per_piece * drafts, depth)
    def attention(first, count, before):
        if halves_held == 1:
            return whole[:, first * drafts : (first + count) * drafts]
        q = after(queries, before)
        return attend(q, cache_keys, cache_values, new_kv, cache_lens, first, count, pieces, drafts)

    def chain_of(blocks, before=()):
        blocks = [after(blocks[0], *before)] + list(blocks[1:]) if before else blocks
        return Chain(ring, project(ring.relative, blocks, out_weight))

    by_chip = lax.axis_size("row") == 4
    first = attention(0, early_beams, queries)
    if by_chip:
        far = partner(first, "row", 1)
        near = partner(first, "row", 0)
        second = attention(early_beams, per_piece - early_beams, first)
        second_far = partner(second, "row", 1)
        second_near = partner(second, "row", 0)
        far = after(far, second)
        early = [first, near, far, partner(far, "row", 0)]
    else:
        early = gather_rows(first)
    chain_one = chain_of(early)
    sent = chain_one.advance()
    kept = kept_rows(after(new_kv, *sent), accepted, dest, beams_here, drafts)
    if by_chip:
        second_far = after(second_far, *sent)
        late = [second, second_near, second_far, partner(second_far, "row", 0)]
        kept_far = partner(kept, "row", 1)
        kept_near = partner(kept, "row", 0)
    else:
        late = gather_rows(attention(early_beams, per_piece - early_beams, first))
        kept = gather_rows(kept)
    half = ring.count // 2
    sides = []
    for word in order_of_work:
        if word == "one":
            sent = chain_one.advance(sent)
        elif word == "product":
            blocks = [after(late[0], *sent)] + late[1:]
            partials = project_side(ring.relative, blocks, out_weight, len(sides))
            sides.append(SideChain(ring, partials, not sides))
            sides[-1].advance()
            sent = partials[:1]
        elif word == "kept" and by_chip:
            kept_far, kept_near = lax.optimization_barrier((kept_far, kept_near, *sent))[:2]
            sent = (*sent, kept_far, kept_near)
            kept = [kept, kept_near, kept_far, partner(kept_far, "row", 0)]
        elif word in ("0", "1"):
            sent = sides[int(word)].advance(sent)
    for step in range(chain_one.step, half):
        sent = chain_one.advance(sent)
    for step in range(1, half):
        for side in range(2):
            if sides[side].step == step:
                sent = sides[side].advance(sent)
    kept[-1] = after(kept[-1], *sent)
    next_kv = place_rows(kept, beams_here, drafts, new_kv.shape[1])
    done = [chain_one.finish(sent)]
    done.append(sides[0].finish(done[:1]))
    done.append(sides[1].finish(done[1:]))
    mixed = jnp.concatenate([done[0], jnp.concatenate(done[1:], 1)], 0)
    return (mixed, next_kv)


def solution(mesh):
    placed = (
        P("row", "mp"),
        P("row", "mp"),
        P("row", "mp", None, None),
        P("row", "mp", None, None),
        P("row"),
        P("row"),
        P("row"),
        P("mp", "row"),
    )
    return jax.shard_map(
        shards,
        mesh=mesh,
        in_specs=placed,
        out_specs=(P("mp", "row"), P("row", None, "mp")),
        check_vma=False,
    )
```

```python
import functools

import jax
import jax.numpy as jnp
from jax import lax
from jax.experimental import pallas as pl
from jax.experimental.pallas import tpu as pltpu
from jax.sharding import PartitionSpec as P

masked_score = -1e30
vmem_bytes = 60 * 2**20
early_beams = 8
order_of_work = ("one", "product", "kept", "one", "product", "0", "one")


def partner(block, axis, bit):
    count = lax.axis_size(axis)
    route = []
    for low in range(count):
        high = low | 1 << bit
        if high != low and high < count:
            route += [(low, high), (high, low)]
    return lax.ppermute(block, axis, route)


def head_slice(values, start, count):
    return lax.dynamic_slice_in_dim(values, start, count, 3)


def attention_kernel(scale, first, count, drafts, group, ahead, lens, q, k, v, fresh, out,
                     q_raw, q_wide, f_raw, f_wide, o_wide, k_held, v_held, order, f_sem, q_sems, k_sems, v_sems):
    halves = out.shape[0]
    size = k.shape[2]
    span = k.shape[1]
    heads = q.shape[1] // size
    stride = k.shape[0] // halves
    block = 2 * size
    most = span // block
    beams = halves * count
    groups = beams // group
    low = first * drafts // 16 * 16
    shift = first * drafts - low
    taken = q_raw.shape[1]
    rows = heads * drafts

    def half_of(i):
        return sum((i >= h * count).astype(jnp.int32) for h in range(1, halves))

    def beam_of(i):
        return i + half_of(i) * (stride - count) + first

    def blocks_of(i):
        return sum((lens[beam_of(i)] + drafts > c * block).astype(jnp.int32) for c in range(1, most)) + 1

    def tally(i, totals):
        held = blocks_of(i)
        return tuple(total + (held <= c + 1).astype(jnp.int32) for c, total in enumerate(totals))

    def rank(i, starts):
        held = blocks_of(i)
        spot = starts[0]
        for c in range(1, most):
            spot = jnp.where(held == c + 1, starts[c], spot)
        order[spot] = i
        return tuple(start + (held == c + 1).astype(jnp.int32) for c, start in enumerate(starts))

    def copies(g, c):
        part = pl.ds(0, c * block)
        for m in range(group):
            at = g * group + m
            beam = beam_of(order[at])
            yield pltpu.make_async_copy(k.at[beam, part], k_held.at[at, part], k_sems.at[at])
            yield pltpu.make_async_copy(v.at[beam, part], v_held.at[at, part], v_sems.at[at])

    def by_length(g, do):
        held = blocks_of(order[g * group + group - 1])
        for c in range(1, most + 1):
            pl.when(held == c)(functools.partial(do, g, c))

    def begin(g, c):
        for copy in copies(g, c):
            copy.start()

    def query_copy(h):
        start = h * stride * drafts + low
        return pltpu.make_async_copy(q.at[pl.ds(start, taken)], q_raw.at[h], q_sems.at[h])

    fresh_copy = pltpu.make_async_copy(fresh, f_raw, f_sem)
    fresh_copy.start()
    for h in range(halves):
        query_copy(h).start()
    totals = lax.fori_loop(0, beams, tally, (jnp.int32(0),) * most, unroll=8)
    lax.fori_loop(0, beams, rank, (jnp.int32(0),) + totals[:-1], unroll=8)
    ahead = min(ahead, groups)
    for g in range(ahead):
        by_length(g, begin)
    fresh_copy.wait()
    for side in range(2):
        f_wide[side, : fresh.shape[0]] = f_raw[:, side * size : (side + 1) * size].astype(jnp.float32)
        f_wide[side, fresh.shape[0] :] = jnp.zeros((8, size), jnp.float32)
    for h in range(halves):
        query_copy(h).wait()
        q_wide[h] = q_raw[h].astype(jnp.float32).reshape(taken, heads, size)

    draft = lax.broadcasted_iota(jnp.int32, (2 * rows, 1), 0) % rows // heads
    upper = lax.broadcasted_iota(jnp.int32, (2 * rows, 1), 0) < rows
    window = 32
    spot = lax.broadcasted_iota(jnp.int32, (window, 1), 0)
    contract = (((1,), (1,)), ((), ()))
    blank = jnp.zeros((rows, size), jnp.bfloat16)

    def attend_group(g, c):
        width = c * block
        for copy in copies(g, c):
            copy.wait()
        chosen = []
        for m in range(group):
            i = g * group + m
            picked = order[i]
            half, beam = half_of(picked), beam_of(picked)
            length = lens[beam]
            at = jnp.minimum(lax.shift_left(lax.shift_right_logical(length, 4), 4), width - window)
            at = pl.multiple_of(at, 16)
            there = length - at
            inside = (spot >= there) & (spot < there + drafts)
            for side, held in enumerate((k_held, v_held)):
                new = f_wide[side, pl.ds(beam * drafts, 8), :]
                new = jnp.concatenate([new, jnp.zeros((window - 8, size), jnp.float32)], 0)
                new = pltpu.roll(new, there, 0).astype(jnp.bfloat16)
                old = held[i, pl.ds(at, window), :]
                held[i, pl.ds(at, window), :] = jnp.where(inside, new, old)
            chosen.append((i, length, half, (picked - half * count) * drafts))
        spots = lax.broadcasted_iota(jnp.int32, (1, width), 1)
        scores, limits = [], []
        for one, two in zip(chosen[::2], chosen[1::2]):
            qs = [
                q_wide[half, pl.ds(shift + row, drafts)].reshape(rows, size).astype(jnp.bfloat16)
                for _, _, half, row in (one, two)
            ]
            left = jnp.concatenate(
                [jnp.concatenate([qs[0], blank], 1), jnp.concatenate([blank, qs[1]], 1)], 0
            )
            keys = jnp.concatenate([k_held[one[0], :width], k_held[two[0], :width]], 1)
            scores.append(lax.dot_general(left, keys, contract, preferred_element_type=jnp.float32))
            limits.append(jnp.where(upper, one[1], two[1]) + draft)
        weights = []
        for s, limit in zip(scores, limits):
            s = jnp.where(spots <= limit, s, masked_score)
            top = jnp.max(s, 1, keepdims=True)
            w = jnp.exp2((s - top) * (scale * 1.4426950408889634)).astype(jnp.bfloat16)
            weights.append((w, 1.0 / jnp.sum(w.astype(jnp.float32), 1, keepdims=True)))
        totals = []
        for (w, share), one, two in zip(weights, chosen[::2], chosen[1::2]):
            values = jnp.concatenate([v_held[one[0], :width], v_held[two[0], :width]], 1)
            totals.append(jnp.dot(w, values, preferred_element_type=jnp.float32) * share)
        for total, one, two in zip(totals, chosen[::2], chosen[1::2]):
            for m, (_, _, half, row) in enumerate((one, two)):
                part = total[m * rows : (m + 1) * rows, m * size : (m + 1) * size]
                o_wide[half, pl.ds(row, drafts)] = part.reshape(drafts, heads, size)

    def step(g, carry):
        @pl.when(g + ahead < groups)
        def _():
            by_length(jnp.minimum(g + ahead, groups - 1), begin)

        by_length(g, attend_group)
        return carry

    lax.fori_loop(0, groups, step, 0)
    for h in range(halves):
        out[h] = o_wide[h].reshape(out.shape[1], out.shape[2]).astype(out.dtype)


def attend(q, k, v, fresh, lens, first, count, halves, drafts, group=8, ahead=6):
    beams, size = k.shape[0], k.shape[3]
    span = k.shape[1] * k.shape[2]
    columns = q.shape[1]
    heads = columns // size
    stride = beams // halves
    taken = (first + count) * drafts - first * drafts // 16 * 16
    taken = (taken + 15) // 16 * 16
    chosen = halves * count
    group = group if count > 8 else 4
    full = pl.BlockSpec(memory_space=pltpu.VMEM)
    outside = pl.BlockSpec(memory_space=pl.ANY)
    return pl.pallas_call(
        functools.partial(attention_kernel, size**-0.5, first, count, drafts, group, ahead),
        out_shape=jax.ShapeDtypeStruct((halves, count * drafts, columns), jnp.bfloat16),
        in_specs=[pl.BlockSpec(memory_space=pltpu.SMEM), outside, outside, outside, outside],
        out_specs=full,
        scratch_shapes=[
            pltpu.VMEM((halves, taken, columns), jnp.bfloat16),
            pltpu.VMEM((halves, taken, heads, size), jnp.float32),
            pltpu.VMEM(fresh.shape, jnp.bfloat16),
            pltpu.VMEM((2, fresh.shape[0] + 8, size), jnp.float32),
            pltpu.VMEM((halves, count * drafts, heads, size), jnp.float32),
            pltpu.VMEM((chosen, span, size), jnp.bfloat16),
            pltpu.VMEM((chosen, span, size), jnp.bfloat16),
            pltpu.SMEM((chosen,), jnp.int32),
            pltpu.SemaphoreType.DMA,
            pltpu.SemaphoreType.DMA((halves,)),
            pltpu.SemaphoreType.DMA((chosen,)),
            pltpu.SemaphoreType.DMA((chosen,)),
        ],
        compiler_params=pltpu.CompilerParams(vmem_limit_bytes=vmem_bytes),
        cost_estimate=pl.CostEstimate(
            flops=4 * halves * count * drafts * columns * span,
            bytes_accessed=4 * halves * count * size * span,
            transcendentals=halves * count * drafts * heads * span,
        ),
    )(lens, q, k.reshape(beams, span, size), v.reshape(beams, span, size), fresh)


def half_attention(queries, new_kv, cache_keys, cache_values, cache_lens):
    beams_here, halves_held, half_length, head_size = cache_keys.shape
    drafts = queries.shape[0] // beams_here
    heads_owned = queries.shape[1] // head_size
    mp_place = lax.axis_index("mp")
    lower_side = mp_place % 2 == 0
    partner_queries, partner_fresh = partner((queries, new_kv), "mp", 0)
    group_queries = jnp.where(
        lower_side,
        jnp.concatenate([queries, partner_queries], 1),
        jnp.concatenate([partner_queries, queries], 1),
    )
    fresh_pair = jnp.where(
        lower_side,
        jnp.concatenate([new_kv, partner_fresh], 1),
        jnp.concatenate([partner_fresh, new_kv], 1),
    )
    group_heads = group_queries.shape[1] // head_size
    sides = (mp_place * halves_held + jnp.arange(halves_held, dtype=jnp.int32)) % 2
    query_block = group_queries.reshape(beams_here, drafts, group_heads, head_size)
    fresh_block = fresh_pair.reshape(beams_here, drafts, 2, head_size)
    fresh_keys = fresh_block[:, :, 0]
    fresh_values = fresh_block[:, :, 1]
    scale = head_size ** (-0.5)
    cache_scores = (
        jnp.einsum("btjd,bsid->bstji", query_block, cache_keys, preferred_element_type=jnp.float32)
        * scale
    )
    fresh_scores = (
        jnp.einsum("btjd,bud->btju", query_block, fresh_keys, preferred_element_type=jnp.float32)
        * scale
    )
    spots = sides[:, None] * half_length + jnp.arange(half_length, dtype=jnp.int32)[None, :]
    cache_valid = (spots[None] < cache_lens[:, None, None])[:, :, None, None, :]
    order = jnp.arange(drafts, dtype=jnp.int32)
    fresh_side = (cache_lens[:, None] + order[None, :]) // half_length
    causal = order[:, None] >= order[None, :]
    fresh_valid = (
        causal[None, None] & (fresh_side[:, None, None, :] == sides[None, :, None, None])
    )[:, :, :, None, :]
    cache_masked = jnp.where(cache_valid, cache_scores, masked_score)
    fresh_masked = jnp.where(fresh_valid, fresh_scores[:, None], masked_score)
    highest = jnp.maximum(jnp.max(cache_masked, -1), jnp.max(fresh_masked, -1))
    cache_weights = jnp.where(cache_valid, jnp.exp(cache_masked - highest[..., None]), 0.0).astype(
        jnp.bfloat16
    )
    fresh_weights = jnp.where(fresh_valid, jnp.exp(fresh_masked - highest[..., None]), 0.0).astype(
        jnp.bfloat16
    )
    partial_value = jnp.einsum(
        "bstji,bsid->bstjd", cache_weights, cache_values, preferred_element_type=jnp.float32
    )
    partial_value = partial_value + jnp.einsum(
        "bstju,bud->bstjd", fresh_weights, fresh_values, preferred_element_type=jnp.float32
    )
    weight_mass = jnp.sum(cache_weights.astype(jnp.float32), -1) + jnp.sum(
        fresh_weights.astype(jnp.float32), -1
    )
    own_start = jnp.where(lower_side, 0, heads_owned).astype(jnp.int32)
    other_start = (heads_owned - own_start).astype(jnp.int32)
    got_partial, got_highest, got_mass = partner(
        (
            head_slice(partial_value, other_start, heads_owned),
            head_slice(highest, other_start, heads_owned),
            head_slice(weight_mass, other_start, heads_owned),
        ),
        "mp",
        0,
    )
    both_partial = jnp.concatenate(
        [head_slice(partial_value, own_start, heads_owned), got_partial], 1
    )
    both_highest = jnp.concatenate([head_slice(highest, own_start, heads_owned), got_highest], 1)
    both_mass = jnp.concatenate([head_slice(weight_mass, own_start, heads_owned), got_mass], 1)
    summit = jnp.max(both_highest, 1)
    factor = jnp.exp(both_highest - summit[:, None])
    numer = jnp.sum(factor[..., None] * both_partial, 1)
    denom = jnp.sum(factor * both_mass, 1)
    return (
        (numer / denom[..., None])
        .astype(jnp.bfloat16)
        .reshape(beams_here * drafts, heads_owned * head_size)
    )


def gather_rows(block):
    count = lax.axis_size("row")
    if count != 4:
        return [lax.all_gather(block, "row", axis=0, tiled=False)[j] for j in range(count)]
    near = partner(block, "row", 0)
    far = partner(block, "row", 1)
    return [block, near, far, partner(far, "row", 0)]


def project_kernel(gathered, pieces, half, table, *refs):
    blocks, weight = refs[:gathered], refs[gathered]
    out, held = refs[gathered + 1 : -1], refs[-1]
    rows = blocks[0].shape[1]
    places = held.shape[0] // rows
    pairs = half - 1
    ahead, back = out[:pairs], out[pairs : 2 * pairs]
    ahead_last, back_last, own_left, own_right = out[2 * pairs :]
    phase = pl.program_id(0) // (pl.num_programs(0) // 2)

    @pl.when(pl.program_id(0) == 0)
    def _():
        for at, block in enumerate(blocks):
            for piece in range(pieces):
                place = table[at * pieces + piece]
                for spot in range(places):

                    @pl.when(place == spot)
                    def _():
                        held[pl.ds(spot * rows, rows)] = block[piece]

    total = jnp.dot(held[...], weight[...], preferred_element_type=jnp.float32)
    total = total.astype(jnp.bfloat16)

    def of(place):
        place = place % places
        return total[place * rows : (place + 1) * rows]

    @pl.when(phase == 0)
    def _():
        for k in range(pairs):
            ahead[k][0] = of(half - k)
            back[k][0] = of(k + 1 - half)
        ahead_last[...] = of(1)
        own_left[...] = of(0)

    @pl.when(phase == 1)
    def _():
        for k in range(pairs):
            ahead[k][0] = of(half - 1 - k)
            back[k][0] = of(k - half)
        back_last[...] = of(-1)
        own_right[...] = of(0)


def project(table, blocks, weight):
    pieces, rows, depth = blocks[0].shape
    places = pieces * len(blocks)
    half = places // 2
    columns = weight.shape[1] // 2
    tile = min(2048, columns)
    tiles = columns // tile
    pair = jax.ShapeDtypeStruct((2, rows, columns), jnp.bfloat16)
    single = jax.ShapeDtypeStruct((rows, columns), jnp.bfloat16)
    ahead = pl.BlockSpec((1, rows, tile), lambda n, t: (n // tiles, 0, n % tiles))
    back = pl.BlockSpec((1, rows, tile), lambda n, t: (1 - n // tiles, 0, n % tiles))
    first = pl.BlockSpec((rows, tile), lambda n, t: (0, jnp.minimum(n, tiles - 1)))
    second = pl.BlockSpec((rows, tile), lambda n, t: (0, jnp.maximum(n - tiles, 0)))
    out = pl.pallas_call(
        functools.partial(project_kernel, len(blocks), pieces, half),
        out_shape=[pair] * (2 * half - 2) + [single] * 4,
        grid_spec=pltpu.PrefetchScalarGridSpec(
            num_scalar_prefetch=1,
            grid=(2 * tiles,),
            in_specs=[pl.BlockSpec((pieces, rows, depth), lambda n, t: (0, 0, 0))] * len(blocks)
            + [pl.BlockSpec((depth, tile), lambda n, t: (0, n))],
            out_specs=[ahead] * (half - 1) + [back] * (half - 1) + [first, second, first, second],
            scratch_shapes=[pltpu.VMEM((places * rows, depth), jnp.bfloat16)],
        ),
        compiler_params=pltpu.CompilerParams(vmem_limit_bytes=vmem_bytes),
        cost_estimate=pl.CostEstimate(
            flops=4 * places * rows * depth * columns,
            bytes_accessed=4 * (places * rows * (depth + columns) + depth * columns),
            transcendentals=0,
        ),
    )(table, *blocks, weight)
    steps = [list(step) for step in zip(out[: half - 1], out[half - 1 : 2 * half - 2])]
    return steps + [list(out[-4:-2])], list(out[-2:])


def project_side_kernel(gathered, pieces, table, *refs):
    blocks, weight = refs[:gathered], refs[gathered]
    out, held = refs[gathered + 1 : -1], refs[-1]
    rows = blocks[0].shape[1]
    places = held.shape[0] // rows

    @pl.when(pl.program_id(0) == 0)
    def _():
        for at, block in enumerate(blocks):
            for piece in range(pieces):
                place = table[at * pieces + piece]
                for spot in range(places):

                    @pl.when(place == spot)
                    def _():
                        held[pl.ds(spot * rows, rows)] = block[piece]

    total = jnp.dot(held[...], weight[...], preferred_element_type=jnp.float32)
    total = total.astype(jnp.bfloat16)
    for spot in range(places):
        out[spot][...] = total[spot * rows : (spot + 1) * rows]


def project_side(table, blocks, weight, side):
    pieces, rows, depth = blocks[0].shape
    columns = weight.shape[1] // 2
    tile = min(512, columns)
    tiles = columns // tile
    places = pieces * len(blocks)
    return pl.pallas_call(
        functools.partial(project_side_kernel, len(blocks), pieces),
        out_shape=[jax.ShapeDtypeStruct((rows, columns), jnp.bfloat16)] * places,
        grid_spec=pltpu.PrefetchScalarGridSpec(
            num_scalar_prefetch=1,
            grid=(tiles,),
            in_specs=[pl.BlockSpec((pieces, rows, depth), lambda n, t: (0, 0, 0))] * len(blocks)
            + [pl.BlockSpec((depth, tile), lambda n, t: (0, n + side * tiles))],
            out_specs=[pl.BlockSpec((rows, tile), lambda n, t: (0, n))] * places,
            scratch_shapes=[pltpu.VMEM((places * rows, depth), jnp.bfloat16)],
        ),
        compiler_params=pltpu.CompilerParams(vmem_limit_bytes=vmem_bytes),
        cost_estimate=pl.CostEstimate(
            flops=2 * places * rows * depth * columns,
            bytes_accessed=2 * (places * rows * (depth + columns) + depth * columns),
            transcendentals=0,
        ),
    )(table, *blocks, weight)


def plus(*blocks):
    return sum(block.astype(jnp.float32) for block in blocks).astype(jnp.bfloat16)


def ring_order(count):
    return list(range(0, count, 2)) + list(range(count - 1, 0, -2))


class Ring:
    def __init__(self):
        count = lax.axis_size("mp")
        order = ring_order(count)
        self.ahead = [(order[i], order[(i + 1) % count]) for i in range(count)]
        self.back = [(b, a) for a, b in self.ahead]
        self.count = count
        rows = lax.axis_size("row")
        slot = jnp.arange(count, dtype=jnp.int32)
        pieces = count // rows
        slot_row = slot // pieces
        if rows == 4:
            slot_row = slot_row ^ lax.axis_index("row")
        owner = slot_row * pieces + slot % pieces
        self.relative = (self.place(owner) - self.place(lax.axis_index("mp"))) % count

    def place(self, device):
        return jnp.where(device % 2 == 0, device // 2, self.count - 1 - device // 2)


class Chain:
    def __init__(self, ring, partials):
        self.ring = ring
        self.partials, self.own = partials
        self.arrived = None
        self.step = 0

    def advance(self, before=()):
        sent = self.partials[self.step]
        if self.arrived is not None:
            arrived = lax.optimization_barrier((*self.arrived, *before))[:2]
            if self.step == len(self.partials) - 1:
                self.own = [plus(self.own[0], arrived[1][1]), plus(self.own[1], arrived[0][1])]
                arrived = [got[0] for got in arrived]
            sent = [plus(own, got) for own, got in zip(sent, arrived)]
        routes = (self.ring.ahead, self.ring.back)
        self.arrived = [lax.ppermute(block, "mp", route) for block, route in zip(sent, routes)]
        self.step += 1
        return sent

    def finish(self, before):
        arrived = lax.optimization_barrier((*self.arrived, *before))[:2]
        return jnp.concatenate([plus(own, got) for own, got in zip(self.own, arrived)], 1)


class SideChain:
    def __init__(self, ring, partials, longer):
        half = ring.count // 2
        self.ring = ring
        self.partials = partials
        self.hops = (half, half - 1) if longer else (half - 1, half)
        self.arrived = []
        self.step = 0

    def advance(self, before=()):
        k, n = self.step, self.ring.count
        places = (self.hops[0] - k, n - self.hops[1] + k)
        arrived = list(self.arrived)
        if arrived:
            arrived = lax.optimization_barrier((*arrived, *before))[:2]
        sent, self.arrived = [], []
        for way, route in enumerate((self.ring.ahead, self.ring.back)):
            if k < self.hops[way]:
                own = self.partials[places[way]]
                own = plus(own, arrived[way]) if arrived else own
                sent.append(own)
                self.arrived.append(lax.ppermute(own, "mp", route))
            else:
                self.arrived.append(arrived[way])
        self.step += 1
        return sent

    def finish(self, before):
        arrived = lax.optimization_barrier((*self.arrived, *before))[:2]
        return plus(self.partials[0], *arrived)


def kept_rows(new_kv, accepted, dest, beams_here, drafts):
    columns = new_kv.shape[1]
    fresh_rows = new_kv.reshape(beams_here, drafts, columns)
    order = jnp.arange(drafts, dtype=jnp.int32)
    kept_mask = order[None, :] < accepted[:, None]
    kept = jnp.where(kept_mask[..., None], fresh_rows, jnp.zeros_like(fresh_rows))
    labels = jnp.stack([dest // beams_here, dest % beams_here], 1).astype(jnp.bfloat16)
    labels = jnp.pad(labels, ((0, 0), (0, 126)))
    return jnp.concatenate([kept.reshape(beams_here, drafts * columns), labels], 1)


def place_rows(gathered, beams_here, drafts, columns):
    width = drafts * columns
    all_rows = jnp.concatenate(gathered, 0)
    places = all_rows[:, width : width + 2].astype(jnp.int32)
    all_dest = places[:, 0] * beams_here + places[:, 1]
    slot = lax.axis_index("row") * beams_here + jnp.arange(beams_here, dtype=jnp.int32)
    placer = (all_dest[None, :] == slot[:, None]).astype(jnp.bfloat16)
    next_kv = jnp.dot(placer, all_rows[:, :width], preferred_element_type=jnp.float32)
    return next_kv.astype(jnp.bfloat16).reshape(beams_here, drafts, columns)


def after(value, *others):
    return lax.optimization_barrier((value, *others))[0]


def shards(queries, new_kv, cache_keys, cache_values, cache_lens, accepted, dest, out_weight):
    beams_here, halves_held, half_length, head_size = cache_keys.shape
    drafts = queries.shape[0] // beams_here
    depth = queries.shape[1]
    pieces = lax.axis_size("mp") // lax.axis_size("row")
    per_piece = beams_here // pieces
    ring = Ring()
    if halves_held == 1:
        whole = half_attention(queries, new_kv, cache_keys, cache_values, cache_lens)
        whole = whole.reshape(pieces, per_piece * drafts, depth)
    def attention(first, count, before):
        if halves_held == 1:
            return whole[:, first * drafts : (first + count) * drafts]
        q = after(queries, before)
        return attend(q, cache_keys, cache_values, new_kv, cache_lens, first, count, pieces, drafts)

    def chain_of(blocks, before=()):
        blocks = [after(blocks[0], *before)] + list(blocks[1:]) if before else blocks
        return Chain(ring, project(ring.relative, blocks, out_weight))

    by_chip = lax.axis_size("row") == 4
    first = attention(0, early_beams, queries)
    if by_chip:
        far = partner(first, "row", 1)
        near = partner(first, "row", 0)
        second = attention(early_beams, per_piece - early_beams, first)
        second_far = partner(second, "row", 1)
        second_near = partner(second, "row", 0)
        far = after(far, second)
        early = [first, near, far, partner(far, "row", 0)]
    else:
        early = gather_rows(first)
    chain_one = chain_of(early)
    sent = chain_one.advance()
    kept = kept_rows(after(new_kv, *sent), accepted, dest, beams_here, drafts)
    if by_chip:
        second_far = after(second_far, *sent)
        late = [second, second_near, second_far, partner(second_far, "row", 0)]
        kept_far = partner(kept, "row", 1)
        kept_near = partner(kept, "row", 0)
    else:
        late = gather_rows(attention(early_beams, per_piece - early_beams, first))
        kept = gather_rows(kept)
    half = ring.count // 2
    sides = []
    for word in order_of_work:
        if word == "one":
            sent = chain_one.advance(sent)
        elif word == "product":
            blocks = [after(late[0], *sent)] + late[1:]
            partials = project_side(ring.relative, blocks, out_weight, len(sides))
            sides.append(SideChain(ring, partials, not sides))
            sides[-1].advance()
            sent = partials[:1]
        elif word == "kept" and by_chip:
            kept_far, kept_near = lax.optimization_barrier((kept_far, kept_near, *sent))[:2]
            sent = (*sent, kept_far, kept_near)
            kept = [kept, kept_near, kept_far, partner(kept_far, "row", 0)]
        elif word in ("0", "1"):
            sent = sides[int(word)].advance(sent)
    for step in range(chain_one.step, half):
        sent = chain_one.advance(sent)
    for step in range(1, half):
        for side in range(2):
            if sides[side].step == step:
                sent = sides[side].advance(sent)
    kept[-1] = after(kept[-1], *sent)
    next_kv = place_rows(kept, beams_here, drafts, new_kv.shape[1])
    done = [chain_one.finish(sent)]
    done.append(sides[0].finish(done[:1]))
    done.append(sides[1].finish(done[1:]))
    mixed = jnp.concatenate([done[0], jnp.concatenate(done[1:], 1)], 0)
    return (mixed, next_kv)


def solution(mesh):
    placed = (
        P("row", "mp"),
        P("row", "mp"),
        P("row", "mp", None, None),
        P("row", "mp", None, None),
        P("row"),
        P("row"),
        P("row"),
        P("mp", "row"),
    )
    return jax.shard_map(
        shards,
        mesh=mesh,
        in_specs=placed,
        out_specs=(P("mp", "row"), P("row", None, "mp")),
        check_vma=False,
    )
```
